512 devices in a mesh: wide: 64 (over x, z), mp: 8 (over y, core).
Axes of the slice: x: 4, y: 4, z: 16, core: 2. Of those that a mesh axis runs over, the one named last changes fastest.
Arguments:
- inputs: bfloat16 [2, 128, 16384], P(None, None, 'wide'), may hold values from -6 to 6
- attn_gain: bfloat16 [16384], P('wide'), may hold values from 0.25 to 1.75
- w_query: bfloat16 [16384, 16384], P('wide', 'mp'), may hold values from -0.0473929 to 0.0473929
- w_keyval: bfloat16 [16384, 8, 256], P('wide', 'mp'), may hold values from -0.046875 to 0.046875
- w_out: bfloat16 [16384, 16384], P('mp', 'wide'), may hold values from -0.046875 to 0.046875
- ffn_gain: bfloat16 [16384], P('wide'), may hold values from 0.25 to 1.75
- w_gateup: bfloat16 [16384, 2, 6656], P('wide', None, 'mp'), may hold values from -0.046875 to 0.046875
- w_down: bfloat16 [6656, 16384], P('mp', 'wide'), may hold values from -0.078125 to 0.078125
- kv_cache: bfloat16 [128, 768, 8, 256], P('wide', None, 'mp'), may hold values from -11 to 11
- lengths: int32 [128], P('wide'), may hold values from 1 to 768, as said below
- positions: int32 [128], P('wide'), may hold values from 768 to 3071
Outputs:
- outputs: bfloat16 [2, 128, 16384], P(None, None, 'wide')
- new_entries: bfloat16 [2, 128, 8, 256], P(None, 'wide', 'mp')
The draws below stay inside these ranges and needn't reach their ends.
Inputs may be any that keep to these rules, and one draw needn't show every extreme that they name: `lengths`: some row has exactly 768 valid positions and some row exactly 1.
All inputs are finite; a program needn't handle non-finite values.
Results may differ from the reference program's by a relative error of at most 0.012.
Values may be sent and summed in bfloat16 or wider, within the bound.
No kernel may reach another device: no remote copies, remote signals or barrier semaphores. Data moves between devices by JAX's collectives and lax.ppermute only.
A program may use at most 64 MiB of HBM per device.

```python
import jax
import jax.numpy as jnp
from jax import lax

D = 16384
NQ = 128
KVH = 8
HD = 128
FF = 6656
STEPS = 2
MAXLEN = 768
ROWS = 128


def row_lengths(key):
    key = jax.random.fold_in(key, 7)
    first_key, second_key, third_key, fourth_key = jax.random.split(key, 4)
    first_draw = jax.random.randint(first_key, (ROWS,), 1, MAXLEN + 1)
    second_draw = jax.random.randint(second_key, (ROWS,), 1, MAXLEN + 1)
    drawn = jnp.minimum(first_draw, second_draw)
    longest_row = jax.random.randint(third_key, (), 0, ROWS)
    shortest_row = (longest_row + 1 + jax.random.randint(fourth_key, (), 0, ROWS - 1)) % ROWS
    row_ids = jnp.arange(ROWS)
    drawn = jnp.where(row_ids == longest_row, MAXLEN, drawn)
    drawn = jnp.where(row_ids == shortest_row, 1, drawn)
    return drawn.astype(jnp.int32)


def draw_lengths(key, part):
    drawn = row_lengths(key)
    return drawn


def draw_inputs(key, part):
    own_key = jax.random.fold_in(key, 21)
    values = jax.random.truncated_normal(own_key, -6.0, 6.0, (STEPS, ROWS, D), jnp.float32)
    return values.astype(jnp.bfloat16)


def draw_w_query(key, part):
    own_key = jax.random.fold_in(key, 22)
    weights = jax.random.truncated_normal(own_key, -6.0, 6.0, (D, NQ * HD), jnp.float32) * D ** (-0.5)
    return weights.astype(jnp.bfloat16)


def draw_kv_cache(key, part):
    own_key = jax.random.fold_in(key, 23)
    cache = jax.random.truncated_normal(own_key, -6.0, 6.0, (ROWS, MAXLEN, KVH, 2 * HD), jnp.float32)
    return cache.astype(jnp.bfloat16)


def place_ends(array, key, least, high):
    dims = array.shape
    index_at = [jax.random.randint(jax.random.fold_in(key, axis), (), 0, dims[axis]) for axis in range(len(dims))]
    array = array.at[tuple(index_at)].set(least)
    longest = dims.index(max(dims))
    index_at[longest] = (index_at[longest] + 1) % dims[longest]
    return array.at[tuple(index_at)].set(high)


def steps_of(key, extent, cuts, smallest, top_value):
    def one(axis_at, blocks):
        heights = jax.random.uniform(jax.random.fold_in(jax.random.fold_in(key, 6), axis_at), (blocks,), jnp.float32, smallest / len(cuts), top_value / len(cuts))
        return jnp.repeat(jnp.exp(heights), extent[axis_at] // blocks).reshape((-1,) + (1,) * (len(extent) - axis_at - 1))

    factor_of = one(*cuts[0])
    for cut in cuts[1:]:
        factor_of = factor_of * one(*cut)
    return factor_of


def normal_values(stream_key, dims, width, limit, shards=(), kind=jnp.bfloat16):
    level = steps_of(stream_key, dims, shards, -0.22, 0.18) if shards else 1.0
    values = jax.random.normal(stream_key, dims, jnp.float32) * width * level
    return jnp.minimum(jnp.maximum(values, -limit), limit).astype(kind)


def setup_inputs(seed: int = 0) -> dict:
    key_of = jax.random.split(jax.random.key(seed), 12)
    inputs = draw_inputs(jax.random.fold_in(key_of[11], 71), 0)
    attn_gain = jnp.clip(1.0 + 0.15 * jax.random.normal(key_of[1], (D,), jnp.float32), 0.25, 1.75).astype(jnp.bfloat16)
    w_query = draw_w_query(jax.random.fold_in(key_of[11], 71), 0)
    w_keyval = normal_values(key_of[3], (D, KVH, 2 * HD), D ** -0.5, 0.046875, ((0, 64), (1, 8)))
    w_out = normal_values(key_of[4], (NQ * HD, D), (NQ * HD) ** -0.5, 0.046875, ((0, 8), (1, 64)))
    ffn_gain = jnp.clip(1.0 + 0.15 * jax.random.normal(key_of[5], (D,), jnp.float32), 0.25, 1.75).astype(jnp.bfloat16)
    w_gateup = normal_values(key_of[6], (D, 2, FF), D ** -0.5, 0.046875, ((0, 64), (2, 8)))
    w_down = normal_values(key_of[7], (FF, D), FF ** -0.5, 0.078125, ((0, 8), (1, 64)))
    kv_cache = draw_kv_cache(jax.random.fold_in(key_of[11], 71), 0)
    lengths = draw_lengths(jax.random.fold_in(key_of[11], 71), 0)
    positions = place_ends(jax.random.randint(key_of[10], (ROWS,), MAXLEN, 4 * MAXLEN), jax.random.fold_in(key_of[10], 1), MAXLEN, (4 * MAXLEN) - 1).astype(jnp.int32)
    return {"inputs": inputs, "attn_gain": attn_gain, "w_query": w_query, "w_keyval": w_keyval, "w_out": w_out, "ffn_gain": ffn_gain, "w_gateup": w_gateup, "w_down": w_down, "kv_cache": kv_cache, "lengths": lengths, "positions": positions}


epsilon = 1e-05
rope_base = 500000.0
masked_score = -1e+30

def rotate(vectors, offsets):
    half_size = vectors.shape[-1] // 2
    freqs = rope_base ** (-(jnp.arange(half_size, dtype=jnp.float32) * 2.0 / vectors.shape[-1]))
    angles = offsets.astype(jnp.float32)[..., None] * freqs
    cosine = jnp.cos(angles)
    sine = jnp.sin(angles)
    first_half = vectors[..., :half_size]
    second_half = vectors[..., half_size:]
    return jnp.concatenate([first_half * cosine - second_half * sine, second_half * cosine + first_half * sine], axis=-1)

def rms_scale(values, gain):
    return values * lax.rsqrt(lax.optimization_barrier(jnp.mean(values * values, axis=-1, keepdims=True)) + epsilon) * gain.astype(jnp.float32)

def attend_row(operands):
    query_row, cache_row, length, fresh = operands
    score_scale = HD ** (-0.5)
    grouped = query_row.astype(jnp.float32).reshape(KVH, NQ // KVH, HD)
    cache_keys = cache_row[..., :HD].astype(jnp.float32)
    cache_values = cache_row[..., HD:].astype(jnp.float32)
    fresh_keys = fresh[..., :HD].astype(jnp.float32)
    fresh_values = fresh[..., HD:].astype(jnp.float32)
    scores = jnp.einsum('kgd,lkd->kgl', grouped, cache_keys) * score_scale
    live = jnp.arange(MAXLEN) < length
    scores = jnp.where(live[None, None, :], scores, masked_score)
    fresh_scores = jnp.einsum('kgd,tkd->kgt', grouped, fresh_keys) * score_scale
    highest = jnp.maximum(lax.optimization_barrier(jnp.max(scores, axis=-1)), lax.optimization_barrier(jnp.max(fresh_scores, axis=-1)))[..., None]
    cache_weights = jnp.exp(scores - highest)
    fresh_weights = jnp.exp(fresh_scores - highest)
    total = lax.optimization_barrier(jnp.sum(cache_weights, axis=-1, keepdims=True)) + lax.optimization_barrier(jnp.sum(fresh_weights, axis=-1, keepdims=True))
    cache_probs = (cache_weights / total).astype(jnp.bfloat16)
    fresh_probs = (fresh_weights / total).astype(jnp.bfloat16)
    mixed = jnp.einsum('kgl,lkd->kgd', cache_probs.astype(jnp.float32), cache_values)
    mixed = mixed + jnp.einsum('kgt,tkd->kgd', fresh_probs.astype(jnp.float32), fresh_values)
    return mixed.astype(jnp.bfloat16).reshape(NQ * HD)

def reference(inputs, attn_gain, w_query, w_keyval, w_out, ffn_gain, w_gateup, w_down, kv_cache, lengths, positions):
    query_weight = w_query.reshape(D, NQ * HD)
    keyval_weight = w_keyval.reshape(D, KVH * 2 * HD)
    gateup_weight = w_gateup.reshape(D, 2 * FF)
    fresh_list = []
    output_list = []
    for step_index in range(STEPS):
        current = inputs[step_index].astype(jnp.float32)
        normed = rms_scale(current, attn_gain).astype(jnp.bfloat16)
        query_sum = jnp.dot(normed, query_weight, preferred_element_type=jnp.float32).reshape(ROWS, NQ, HD)
        keyval_sum = jnp.dot(normed, keyval_weight, preferred_element_type=jnp.float32).reshape(ROWS, KVH, 2 * HD)
        offsets = (positions + step_index)[:, None]
        queries = rotate(query_sum, offsets).astype(jnp.bfloat16)
        keys_new = rotate(keyval_sum[..., :HD], offsets).astype(jnp.bfloat16)
        values_new = keyval_sum[..., HD:].astype(jnp.bfloat16)
        fresh_list.append(jnp.concatenate([keys_new, values_new], axis=-1))
        fresh = jnp.stack(fresh_list, axis=1)
        heads = lax.map(attend_row, (queries, kv_cache, lengths, fresh))
        hidden_state = current + jnp.dot(heads, w_out, preferred_element_type=jnp.float32)
        ffn_in = rms_scale(hidden_state, ffn_gain).astype(jnp.bfloat16)
        gateup = jnp.dot(ffn_in, gateup_weight, preferred_element_type=jnp.float32)
        activated = (jax.nn.silu(gateup[:, :FF]) * gateup[:, FF:]).astype(jnp.bfloat16)
        result = hidden_state + jnp.dot(activated, w_down, preferred_element_type=jnp.float32)
        output_list.append(result.astype(jnp.bfloat16))
    return (jnp.stack(output_list), jnp.stack(fresh_list))
```

```python
import jax
import jax.numpy as jnp
from jax import lax
from jax.sharding import Mesh, PartitionSpec as P

D = 16384
STEPS = 2

epsilon = 1e-05
rope_base = 500000.0
masked_score = -1e30

WIDE = ("x", "zh", "zl")
MP = ("y", "core")
REDUCE_ORDER = ("x", "zl", "zh")
GATHER_ORDER = ("zh", "zl", "x")
SIZES = {"x": 4, "zh": 4, "zl": 4, "y": 4, "core": 2}


def rotate(vectors, offsets):
    half_size = vectors.shape[-1] // 2
    freqs = rope_base ** (-(jnp.arange(half_size, dtype=jnp.float32) * 2.0 / vectors.shape[-1]))
    angles = offsets.astype(jnp.float32)[..., None] * freqs
    cosine = jnp.cos(angles)
    sine = jnp.sin(angles)
    first_half = vectors[..., :half_size]
    second_half = vectors[..., half_size:]
    return jnp.concatenate(
        [first_half * cosine - second_half * sine, second_half * cosine + first_half * sine],
        axis=-1,
    )


def exchange(blocks, axis):
    return lax.all_to_all(blocks, axis, 0, 0, tiled=True)


def spread_sum(terms):
    rows, columns = terms.shape
    for axis in REDUCE_ORDER:
        size = SIZES[axis]
        rows //= size
        received = exchange(terms.astype(jnp.bfloat16).reshape(size, rows, columns), axis)
        terms = jnp.sum(received.astype(jnp.float32), axis=0)
    return terms


def collect(block):
    for axis in GATHER_ORDER:
        size = SIZES[axis]
        rows, columns = block.shape
        copies = jnp.broadcast_to(block[None], (size, rows, columns))
        block = exchange(copies, axis).reshape(size * rows, columns)
    return block


def group_sum(terms, base):
    rows, columns = terms.shape
    received = exchange(terms.astype(jnp.bfloat16).reshape(8, rows // 8, columns), MP)
    return base + jnp.sum(received.astype(jnp.float32), axis=0)


def group_collect(block):
    rows, columns = block.shape
    copies = jnp.broadcast_to(block[None], (8, rows, columns))
    return exchange(copies, MP).reshape(8 * rows, columns)


def lane_squares(values):
    squares = values * values
    return squares[:, :128] + squares[:, 128:]


def attend(queries, kv_cache, lengths, fresh_keys, fresh_values, score_scale):
    rows, steps, heads, head_dim = queries.shape
    merged = queries.reshape(rows, steps * heads, head_dim)
    scores = (
        jnp.einsum("rgd,rld->rgl", merged, kv_cache[..., :head_dim], preferred_element_type=jnp.float32)
        * score_scale
    )
    live = jnp.arange(kv_cache.shape[1])[None, None, :] < lengths[:, None, None]
    scores = jnp.where(live, scores, masked_score)
    fresh_scores = (
        jnp.einsum("rgd,rtd->rgt", merged, fresh_keys, preferred_element_type=jnp.float32) * score_scale
    )
    query_step = jnp.arange(steps * heads) // heads
    seen = jnp.arange(steps)[None, None, :] <= query_step[None, :, None]
    fresh_scores = jnp.where(seen, fresh_scores, masked_score)
    highest = jnp.maximum(jnp.max(scores, axis=-1), jnp.max(fresh_scores, axis=-1))[..., None]
    cache_weights = jnp.exp(scores - highest)
    fresh_weights = jnp.exp(fresh_scores - highest)
    total = jnp.sum(cache_weights, axis=-1, keepdims=True) + jnp.sum(
        fresh_weights, axis=-1, keepdims=True
    )
    cache_probs = (cache_weights / total).astype(jnp.bfloat16)
    fresh_probs = (fresh_weights / total).astype(jnp.bfloat16)
    mixed = jnp.einsum(
        "rgl,rld->rgd", cache_probs, kv_cache[..., head_dim:], preferred_element_type=jnp.float32
    ) + jnp.einsum("rgt,rtd->rgd", fresh_probs, fresh_values, preferred_element_type=jnp.float32)
    return mixed.reshape(rows, steps, heads, head_dim)


def body(
    inputs,
    attn_gain,
    w_query,
    w_keyval,
    w_out,
    ffn_gain,
    w_gateup,
    w_down,
    kv_cache,
    lengths,
    positions,
):
    steps, all_rows, local_width = inputs.shape
    local_rows = kv_cache.shape[0]
    head_dim = kv_cache.shape[3] // 2
    local_queries = w_query.shape[1] // head_dim
    local_hidden = w_down.shape[0]
    score_scale = head_dim ** (-0.5)
    keyval_weight = w_keyval.reshape(local_width, 2 * head_dim)
    gateup_weight = w_gateup.reshape(local_width, 2 * local_hidden)
    keyvals_at = local_queries * head_dim
    squares_at = keyvals_at + 2 * head_dim

    current = (
        inputs.reshape(steps, 4, 4, 4, local_rows, local_width)
        .transpose(1, 3, 2, 0, 4, 5)
        .reshape(steps * all_rows, local_width)
        .astype(jnp.float32)
    )
    scaled = (current * attn_gain.astype(jnp.float32)).astype(jnp.bfloat16)
    terms = jnp.concatenate(
        [
            jnp.dot(scaled, w_query, preferred_element_type=jnp.float32),
            jnp.dot(scaled, keyval_weight, preferred_element_type=jnp.float32),
            lane_squares(current),
        ],
        axis=1,
    )
    sums = spread_sum(terms)
    mean = jnp.sum(sums[:, squares_at:], axis=-1, keepdims=True) / D
    sums = (sums[:, :squares_at] * lax.rsqrt(mean + epsilon)).reshape(steps, local_rows, squares_at)
    offsets = positions[None, :] + jnp.arange(steps)[:, None]
    queries = rotate(
        sums[..., :keyvals_at].reshape(steps, local_rows, local_queries, head_dim), offsets[..., None]
    ).astype(jnp.bfloat16)
    keys_new = rotate(sums[..., keyvals_at : keyvals_at + head_dim], offsets).astype(jnp.bfloat16)
    values_new = sums[..., keyvals_at + head_dim :].astype(jnp.bfloat16)
    new_entries = jnp.concatenate([keys_new, values_new], axis=-1)[:, :, None, :]
    mixed = attend(
        queries.transpose(1, 0, 2, 3),
        kv_cache.reshape(local_rows, -1, 2 * head_dim),
        lengths,
        keys_new.transpose(1, 0, 2),
        values_new.transpose(1, 0, 2),
        score_scale,
    )
    heads = mixed.astype(jnp.bfloat16).transpose(1, 0, 2, 3).reshape(steps * local_rows, keyvals_at)

    attn_terms = jnp.dot(collect(heads), w_out, preferred_element_type=jnp.float32)
    own = lax.axis_index(MP) * (steps * all_rows // 8)
    residual = lax.dynamic_slice_in_dim(current, own, steps * all_rows // 8, axis=0)
    own_state = group_sum(attn_terms, residual)
    hidden_state = group_collect(own_state.astype(jnp.bfloat16)).astype(jnp.float32)
    ffn_in = (hidden_state * ffn_gain.astype(jnp.float32)).astype(jnp.bfloat16)
    gateup_terms = jnp.concatenate(
        [
            jnp.dot(ffn_in, gateup_weight, preferred_element_type=jnp.float32),
            lane_squares(hidden_state),
        ],
        axis=1,
    )
    gateup = spread_sum(gateup_terms)
    mean = jnp.sum(gateup[:, 2 * local_hidden :], axis=-1, keepdims=True) / D
    gateup = gateup[:, : 2 * local_hidden] * lax.rsqrt(mean + epsilon)
    activated = (jax.nn.silu(gateup[:, :local_hidden]) * gateup[:, local_hidden:]).astype(jnp.bfloat16)
    down_terms = jnp.dot(collect(activated), w_down, preferred_element_type=jnp.float32)
    result = group_collect(group_sum(down_terms, own_state).astype(jnp.bfloat16))
    outputs = (
        result.reshape(4, 4, 4, steps, local_rows, local_width)
        .transpose(3, 0, 2, 1, 4, 5)
        .reshape(steps, all_rows, local_width)
    )
    return (outputs, new_entries)


def solution(mesh):
    fine = Mesh(mesh.devices.reshape(4, 4, 4, 4, 2), ("x", "zh", "zl", "y", "core"))
    in_specs = (
        P(None, None, WIDE),
        P(WIDE),
        P(WIDE, MP),
        P(WIDE, MP, None),
        P(MP, WIDE),
        P(WIDE),
        P(WIDE, None, MP),
        P(MP, WIDE),
        P(WIDE, None, MP, None),
        P(WIDE),
        P(WIDE),
    )
    out_specs = (P(None, None, WIDE), P(None, WIDE, MP, None))
    return jax.shard_map(body, mesh=fine, in_specs=in_specs, out_specs=out_specs, check_vma=False)
```

```python
import jax
import jax.numpy as jnp
from jax import lax
from jax.sharding import Mesh, PartitionSpec as P

D = 16384
STEPS = 2

epsilon = 1e-05
rope_base = 500000.0
masked_score = -1e30

WIDE = ("x", "z")
MP = ("y", "core")
XS, ZS, YS, CORES = 4, 16, 4, 2


def rotate(vectors, offsets):
    half_size = vectors.shape[-1] // 2
    freqs = rope_base ** (-(jnp.arange(half_size, dtype=jnp.float32) * 2.0 / vectors.shape[-1]))
    angles = offsets.astype(jnp.float32)[..., None] * freqs
    cosine = jnp.cos(angles)
    sine = jnp.sin(angles)
    first_half = vectors[..., :half_size]
    second_half = vectors[..., half_size:]
    return jnp.concatenate(
        [first_half * cosine - second_half * sine, second_half * cosine + first_half * sine],
        axis=-1,
    )


def exchange(blocks, axis):
    return lax.all_to_all(blocks, axis, 0, 0, tiled=True)


def sum_over(terms, axis, size):
    rows, columns = terms.shape
    received = exchange(terms.astype(jnp.bfloat16).reshape(size, rows // size, columns), axis)
    return jnp.sum(received.astype(jnp.float32), axis=0)


def collect(block, axis, size):
    return exchange(jnp.broadcast_to(block[None], (size,) + block.shape), axis)


def wide_dot(rows, weights):
    return jnp.concatenate(
        [jnp.dot(rows, weights[at], preferred_element_type=jnp.float32) for at in range(XS)], axis=1
    )


def lane_squares(values):
    squares = values * values
    return sum(squares[:, at : at + 128] for at in range(0, values.shape[1], 128))


def attend(queries, kv_cache, lengths, fresh_keys, fresh_values, score_scale):
    rows, steps, heads, head_dim = queries.shape
    merged = queries.reshape(rows, steps * heads, head_dim)
    scores = (
        jnp.einsum("rgd,rld->rgl", merged, kv_cache[..., :head_dim], preferred_element_type=jnp.float32)
        * score_scale
    )
    live = jnp.arange(kv_cache.shape[1])[None, None, :] < lengths[:, None, None]
    scores = jnp.where(live, scores, masked_score)
    fresh_scores = (
        jnp.einsum("rgd,rtd->rgt", merged, fresh_keys, preferred_element_type=jnp.float32) * score_scale
    )
    query_step = jnp.arange(steps * heads) // heads
    seen = jnp.arange(steps)[None, None, :] <= query_step[None, :, None]
    fresh_scores = jnp.where(seen, fresh_scores, masked_score)
    highest = jnp.maximum(jnp.max(scores, axis=-1), jnp.max(fresh_scores, axis=-1))[..., None]
    cache_weights = jnp.exp(scores - highest)
    fresh_weights = jnp.exp(fresh_scores - highest)
    total = jnp.sum(cache_weights, axis=-1, keepdims=True) + jnp.sum(
        fresh_weights, axis=-1, keepdims=True
    )
    cache_probs = (cache_weights / total).astype(jnp.bfloat16)
    fresh_probs = (fresh_weights / total).astype(jnp.bfloat16)
    mixed = jnp.einsum(
        "rgl,rld->rgd", cache_probs, kv_cache[..., head_dim:], preferred_element_type=jnp.float32
    ) + jnp.einsum("rgt,rtd->rgd", fresh_probs, fresh_values, preferred_element_type=jnp.float32)
    return mixed.reshape(rows, steps, heads, head_dim)


def body(
    inputs,
    attn_gain,
    w_query,
    w_keyval,
    w_out,
    ffn_gain,
    w_gateup,
    w_down,
    kv_cache,
    lengths,
    positions,
):
    steps, all_rows, local_width = inputs.shape
    local_rows = kv_cache.shape[0]
    head_dim = kv_cache.shape[3] // 2
    local_queries = w_query.shape[1] // head_dim
    local_hidden = w_down.shape[0]
    score_scale = head_dim ** (-0.5)
    keyval_weight = w_keyval.reshape(local_width, 2 * head_dim)
    gateup_weight = w_gateup.reshape(local_width, 2 * local_hidden)
    keyvals_at = local_queries * head_dim
    squares_at = keyvals_at + 2 * head_dim

    with jax.named_scope("gather_weights"):
        gains = jnp.broadcast_to(ffn_gain[None], (16, local_width))
        lines = jnp.concatenate([inputs.reshape(steps * all_rows, local_width), gains], axis=0)
        lines = lax.all_gather(lines, "x", axis=0, tiled=False)
        out_weights = lax.all_gather(w_out, "x", axis=0, tiled=False)
        gateup_weights = lax.all_gather(gateup_weight, "x", axis=0, tiled=True)
        down_weights = lax.all_gather(w_down, "x", axis=0, tiled=False)

    current = (
        inputs.reshape(steps, XS * ZS, local_rows, local_width)
        .transpose(1, 0, 2, 3)
        .reshape(steps * all_rows, local_width)
        .astype(jnp.float32)
    )
    scaled = (current * attn_gain.astype(jnp.float32)).astype(jnp.bfloat16)
    terms = jnp.concatenate(
        [
            jnp.dot(scaled, w_query, preferred_element_type=jnp.float32),
            jnp.dot(scaled, keyval_weight, preferred_element_type=jnp.float32),
            lane_squares(current),
        ],
        axis=1,
    )
    sums = sum_over(sum_over(terms, "x", XS), "z", ZS)
    mean = jnp.sum(sums[:, squares_at:], axis=-1, keepdims=True) / D
    sums = (sums[:, :squares_at] * lax.rsqrt(mean + epsilon)).reshape(steps, local_rows, squares_at)
    offsets = positions[None, :] + jnp.arange(steps)[:, None]
    queries = rotate(
        sums[..., :keyvals_at].reshape(steps, local_rows, local_queries, head_dim), offsets[..., None]
    ).astype(jnp.bfloat16)
    keys_new = rotate(sums[..., keyvals_at : keyvals_at + head_dim], offsets).astype(jnp.bfloat16)
    values_new = sums[..., keyvals_at + head_dim :].astype(jnp.bfloat16)
    new_entries = jnp.concatenate([keys_new, values_new], axis=-1)[:, :, None, :]
    mixed = attend(
        queries.transpose(1, 0, 2, 3),
        kv_cache.reshape(local_rows, -1, 2 * head_dim),
        lengths,
        keys_new.transpose(1, 0, 2),
        values_new.transpose(1, 0, 2),
        score_scale,
    )
    heads = mixed.astype(jnp.bfloat16).transpose(1, 0, 2, 3).reshape(steps * local_rows, keyvals_at)

    x_rows = steps * all_rows // XS
    half = x_rows // CORES
    width = XS * local_width
    residual = (
        lax.dynamic_index_in_dim(
            lines[:, : steps * all_rows].reshape(XS, steps, XS, CORES, half // (steps * local_rows), local_rows, local_width),
            lax.axis_index("x"), 2, keepdims=False,
        )
    )
    residual = lax.dynamic_index_in_dim(residual, lax.axis_index("core"), 2, keepdims=False)
    residual = residual.transpose(2, 1, 3, 0, 4).reshape(half, width).astype(jnp.float32)
    gain = lines[:, steps * all_rows].reshape(1, width).astype(jnp.float32)

    attn_terms = wide_dot(collect(heads, "z", ZS).reshape(x_rows, keyvals_at), out_weights)
    pair_terms = sum_over(attn_terms, "core", CORES).astype(jnp.bfloat16)
    own_state = residual + jnp.sum(collect(pair_terms, "y", YS).astype(jnp.float32), axis=0)
    hidden_state = lax.all_gather(own_state.astype(jnp.bfloat16), "core", axis=0, tiled=True).astype(jnp.float32)
    ffn_in = (hidden_state * gain).astype(jnp.bfloat16)
    gateup_terms = jnp.concatenate(
        [
            jnp.dot(ffn_in, gateup_weights, preferred_element_type=jnp.float32),
            lane_squares(hidden_state),
        ],
        axis=1,
    )
    gateup = sum_over(gateup_terms, "z", ZS)
    mean = jnp.sum(gateup[:, 2 * local_hidden :], axis=-1, keepdims=True) / D
    gateup = gateup[:, : 2 * local_hidden] * lax.rsqrt(mean + epsilon)
    activated = (jax.nn.silu(gateup[:, :local_hidden]) * gateup[:, local_hidden:]).astype(jnp.bfloat16)
    down_terms = wide_dot(collect(activated, "z", ZS).reshape(x_rows, local_hidden), down_weights)
    pair_terms = (sum_over(down_terms, "core", CORES) + own_state * (1.0 / YS)).astype(jnp.bfloat16)
    blocks = pair_terms.reshape(half, XS, local_width).transpose(1, 0, 2)
    blocks = jnp.broadcast_to(blocks[:, None], (XS, YS, half, local_width))
    received = exchange(blocks.reshape(XS * YS, half, local_width), ("x", "y"))
    result = jnp.sum(received.reshape(XS, YS, half, local_width).astype(jnp.float32), axis=1)
    result = lax.all_gather(result.astype(jnp.bfloat16), "core", axis=0, tiled=False)
    outputs = (
        result.reshape(CORES, XS, half // (steps * local_rows), steps, local_rows, local_width)
        .transpose(3, 1, 0, 2, 4, 5)
        .reshape(steps, all_rows, local_width)
    )
    return (outputs, new_entries)


def solution(mesh):
    fine = Mesh(mesh.devices.reshape(XS, ZS, YS, CORES), ("x", "z", "y", "core"))
    in_specs = (
        P(None, None, WIDE),
        P(WIDE),
        P(WIDE, MP),
        P(WIDE, MP, None),
        P(MP, WIDE),
        P(WIDE),
        P(WIDE, None, MP),
        P(MP, WIDE),
        P(WIDE, None, MP, None),
        P(WIDE),
        P(WIDE),
    )
    out_specs = (P(None, None, WIDE), P(None, WIDE, MP, None))
    return jax.shard_map(body, mesh=fine, in_specs=in_specs, out_specs=out_specs, check_vma=False)
```

```python
import jax
import jax.numpy as jnp
from jax import lax
from jax.sharding import Mesh, PartitionSpec as P

D = 16384
STEPS = 2

epsilon = 1e-05
rope_base = 500000.0
masked_score = -1e30

WIDE = ("x", "z")
MP = ("y", "core")
XS, ZS, YS, CORES = 4, 16, 4, 2


def rotate(vectors, offsets):
    half_size = vectors.shape[-1] // 2
    freqs = rope_base ** (-(jnp.arange(half_size, dtype=jnp.float32) * 2.0 / vectors.shape[-1]))
    angles = offsets.astype(jnp.float32)[..., None] * freqs
    cosine = jnp.cos(angles)
    sine = jnp.sin(angles)
    first_half = vectors[..., :half_size]
    second_half = vectors[..., half_size:]
    return jnp.concatenate(
        [first_half * cosine - second_half * sine, second_half * cosine + first_half * sine],
        axis=-1,
    )


def exchange(blocks, axis):
    return lax.all_to_all(blocks, axis, 0, 0, tiled=True)


def sum_over(terms, axis, size):
    rows, columns = terms.shape
    received = exchange(terms.astype(jnp.bfloat16).reshape(size, rows // size, columns), axis)
    return jnp.sum(received.astype(jnp.float32), axis=0)


def collect(block, axis, size):
    return exchange(jnp.broadcast_to(block[None], (size,) + block.shape), axis)


def shift(block, by):
    return lax.ppermute(block, "x", [(at, (at + by) % XS) for at in range(XS)])


def both_ways(block):
    return shift(block, -1), shift(block, 1)


def far_block(after, before):
    return shift(before[0], 1), shift(after[1], -1)


def core_sum(terms):
    received = exchange(terms.astype(jnp.bfloat16).transpose(1, 0, 2, 3), "core")
    return jnp.sum(received.astype(jnp.float32), axis=0)


def across(blocks):
    shape = blocks.shape
    copies = jnp.broadcast_to(blocks.astype(jnp.bfloat16)[:, None], (XS, YS) + shape[1:])
    received = exchange(copies.reshape((XS * YS,) + shape[1:]), ("x", "y"))
    return jnp.sum(received.reshape((XS, YS) + shape[1:]).astype(jnp.float32), axis=1)


def turn(blocks, by):
    return lax.dynamic_slice_in_dim(jnp.concatenate([blocks, blocks], axis=0), by, XS, axis=0)


def together(*values):
    return lax.optimization_barrier(values)


def lane_squares(values, lanes):
    squares = values * values
    return sum(squares[:, at : at + lanes] for at in range(0, values.shape[1], lanes))


def attend(queries, kv_cache, lengths, fresh_keys, fresh_values, score_scale):
    rows, steps, heads, head_dim = queries.shape
    merged = queries.reshape(rows, steps * heads, head_dim)
    scores = (
        jnp.einsum("rgd,rld->rgl", merged, kv_cache[..., :head_dim], preferred_element_type=jnp.float32)
        * score_scale
    )
    live = jnp.arange(kv_cache.shape[1])[None, None, :] < lengths[:, None, None]
    scores = jnp.where(live, scores, masked_score)
    fresh_scores = (
        jnp.einsum("rgd,rtd->rgt", merged, fresh_keys, preferred_element_type=jnp.float32) * score_scale
    )
    query_step = jnp.arange(steps * heads) // heads
    seen = jnp.arange(steps)[None, None, :] <= query_step[None, :, None]
    fresh_scores = jnp.where(seen, fresh_scores, masked_score)
    highest = jnp.maximum(jnp.max(scores, axis=-1), jnp.max(fresh_scores, axis=-1))[..., None]
    cache_weights = jnp.exp(scores - highest)
    fresh_weights = jnp.exp(fresh_scores - highest)
    total = jnp.sum(cache_weights, axis=-1, keepdims=True) + jnp.sum(
        fresh_weights, axis=-1, keepdims=True
    )
    cache_probs = (cache_weights / total).astype(jnp.bfloat16)
    fresh_probs = (fresh_weights / total).astype(jnp.bfloat16)
    mixed = jnp.einsum(
        "rgl,rld->rgd", cache_probs, kv_cache[..., head_dim:], preferred_element_type=jnp.float32
    ) + jnp.einsum("rgt,rtd->rgd", fresh_probs, fresh_values, preferred_element_type=jnp.float32)
    return mixed.reshape(rows, steps, heads, head_dim)


def body(
    inputs,
    attn_gain,
    w_query,
    w_keyval,
    w_out,
    ffn_gain,
    w_gateup,
    w_down,
    kv_cache,
    lengths,
    positions,
):
    steps, all_rows, local_width = inputs.shape
    local_rows = kv_cache.shape[0]
    head_dim = kv_cache.shape[3] // 2
    local_queries = w_query.shape[1] // head_dim
    local_hidden = w_down.shape[0]
    score_scale = head_dim ** (-0.5)
    keyval_weight = w_keyval.reshape(local_width, 2 * head_dim)
    keyvals_at = local_queries * head_dim
    squares_at = keyvals_at + 2 * head_dim
    rows = steps * all_rows
    x_rows = rows // XS
    half = x_rows // CORES
    gateup = w_gateup.transpose(1, 2, 0).astype(jnp.float32) * ffn_gain.astype(jnp.float32)
    gateup = gateup.astype(jnp.bfloat16)

    current = (
        inputs.reshape(steps, XS, all_rows // XS, local_width)
        .transpose(1, 0, 2, 3)
        .reshape(rows, local_width)
        .astype(jnp.float32)
    )
    scaled = (current * attn_gain.astype(jnp.float32)).astype(jnp.bfloat16)
    terms = jnp.concatenate(
        [
            jnp.dot(scaled, w_query, preferred_element_type=jnp.float32),
            jnp.dot(scaled, keyval_weight, preferred_element_type=jnp.float32),
            lane_squares(current, 128),
        ],
        axis=1,
    )
    sums = sum_over(terms, "x", XS).astype(jnp.bfloat16)
    sums, gateup = together(sums, gateup)
    gateup_after, gateup_before = both_ways(gateup)
    sums = sums.reshape(steps, ZS, local_rows, -1).transpose(1, 0, 2, 3).reshape(x_rows, -1)
    sums = sum_over(sums, "z", ZS)
    sums, gateup_after, gateup_before, w_down = together(sums, gateup_after, gateup_before, w_down)
    gateup_far = far_block(gateup_after, gateup_before)
    down = w_down.reshape(2, local_hidden // 2, local_width)
    down_after, down_before = both_ways(down)
    mean = jnp.sum(sums[:, squares_at:], axis=-1, keepdims=True) / D
    sums = (sums[:, :squares_at] * lax.rsqrt(mean + epsilon)).reshape(steps, local_rows, squares_at)
    offsets = positions[None, :] + jnp.arange(steps)[:, None]
    queries = rotate(
        sums[..., :keyvals_at].reshape(steps, local_rows, local_queries, head_dim), offsets[..., None]
    ).astype(jnp.bfloat16)
    keys_new = rotate(sums[..., keyvals_at : keyvals_at + head_dim], offsets).astype(jnp.bfloat16)
    values_new = sums[..., keyvals_at + head_dim :].astype(jnp.bfloat16)
    new_entries = jnp.concatenate([keys_new, values_new], axis=-1)[:, :, None, :]
    mixed = attend(
        queries.transpose(1, 0, 2, 3),
        kv_cache.reshape(local_rows, -1, 2 * head_dim),
        lengths,
        keys_new.transpose(1, 0, 2),
        values_new.transpose(1, 0, 2),
        score_scale,
    )
    heads = mixed.astype(jnp.bfloat16).transpose(1, 0, 2, 3).reshape(steps * local_rows, keyvals_at)

    all_heads = collect(collect(heads, "z", ZS).reshape(x_rows, keyvals_at), "x", XS)
    all_heads, gateup_far, down_after, down_before = together(
        all_heads, gateup_far, down_after, down_before
    )
    attn_terms = jnp.dot(
        all_heads.reshape(rows, keyvals_at), w_out, preferred_element_type=jnp.float32
    ).reshape(XS, CORES, half, local_width)
    residual = lax.dynamic_index_in_dim(
        inputs.reshape(steps, XS, CORES, ZS // CORES, local_rows, local_width),
        lax.axis_index("core"), 2, keepdims=False,
    )
    residual = residual.transpose(1, 2, 0, 3, 4).reshape(XS, half, local_width).astype(jnp.float32)
    state = across(core_sum(attn_terms) + residual * (1.0 / YS))
    state = turn(state, lax.axis_index("x"))
    ffn_in = lax.all_gather(state.astype(jnp.bfloat16), "core", axis=0, tiled=False)
    ffn_in, w_down = together(ffn_in, w_down)
    ffn_in = ffn_in.transpose(1, 0, 2, 3).reshape(XS, x_rows, local_width)
    squares = ffn_in.astype(jnp.float32)
    squares = jnp.sum(squares * squares, axis=0)
    halves = []
    for part in range(2):
        pieces = (gateup[part], gateup_after[part], gateup_far[part], gateup_before[part])
        halves.append(
            sum(
                lax.dot_general(
                    ffn_in[at], piece, (((1,), (1,)), ((), ())), preferred_element_type=jnp.float32
                )
                for at, piece in enumerate(pieces)
            )
        )
        lanes = squares[:, 128 * part : 128 * part + 128]
        halves.append(lanes[:, :64] + lanes[:, 64:])
    terms = jnp.concatenate(halves, axis=1).astype(jnp.bfloat16)
    terms, down_after, down_before = together(terms, down_after, down_before)
    down_far = far_block(down_after, down_before)
    sums = sum_over(terms, "z", ZS)
    sums, down_far = together(sums, down_far)
    padded = local_hidden + 64
    gate, up = sums[:, :padded], sums[:, padded:]
    mean = jnp.sum(gate[:, local_hidden:] + up[:, local_hidden:], axis=-1, keepdims=True) / D
    scale = lax.rsqrt(mean + epsilon)
    activated = jax.nn.silu(gate[:, :local_hidden] * scale) * (up[:, :local_hidden] * scale)
    hidden = collect(activated.astype(jnp.bfloat16), "z", ZS).reshape(x_rows, local_hidden)
    pieces = (
        w_down,
        down_after.reshape(local_hidden, local_width),
        jnp.concatenate(down_far, axis=0),
        down_before.reshape(local_hidden, local_width),
    )
    down_terms = jnp.stack(
        [jnp.dot(hidden, piece, preferred_element_type=jnp.float32) for piece in pieces]
    ).reshape(XS, CORES, half, local_width)
    last = core_sum(down_terms) + state * (1.0 / YS)
    result = across(turn(last.astype(jnp.bfloat16), (XS - lax.axis_index("x")) % XS))
    result = lax.all_gather(result.astype(jnp.bfloat16), "core", axis=0, tiled=False)
    outputs = (
        result.reshape(CORES, XS, half // (steps * local_rows), steps, local_rows, local_width)
        .transpose(3, 1, 0, 2, 4, 5)
        .reshape(steps, all_rows, local_width)
    )
    return (outputs, new_entries)


def solution(mesh):
    fine = Mesh(mesh.devices.reshape(XS, ZS, YS, CORES), ("x", "z", "y", "core"))
    in_specs = (
        P(None, None, WIDE),
        P(WIDE),
        P(WIDE, MP),
        P(WIDE, MP, None),
        P(MP, WIDE),
        P(WIDE),
        P(WIDE, None, MP),
        P(MP, WIDE),
        P(WIDE, None, MP, None),
        P(WIDE),
        P(WIDE),
    )
    out_specs = (P(None, None, WIDE), P(None, WIDE, MP, None))
    return jax.shard_map(body, mesh=fine, in_specs=in_specs, out_specs=out_specs, check_vma=False)
```

```python
import jax
import jax.numpy as jnp
from jax import lax
from jax.sharding import Mesh, PartitionSpec as P

D = 16384
STEPS = 2

epsilon = 1e-05
rope_base = 500000.0
masked_score = -1e30

WIDE = ("x", "z")
MP = ("y", "core")
XS, ZS, YS, CORES = 4, 16, 4, 2


def rotate(vectors, offsets):
    half_size = vectors.shape[-1] // 2
    freqs = rope_base ** (-(jnp.arange(half_size, dtype=jnp.float32) * 2.0 / vectors.shape[-1]))
    angles = offsets.astype(jnp.float32)[..., None] * freqs
    cosine = jnp.cos(angles)
    sine = jnp.sin(angles)
    first_half = vectors[..., :half_size]
    second_half = vectors[..., half_size:]
    return jnp.concatenate(
        [first_half * cosine - second_half * sine, second_half * cosine + first_half * sine],
        axis=-1,
    )


def exchange(blocks, axis):
    return lax.all_to_all(blocks, axis, 0, 0, tiled=True)


def sum_over(terms, axis, size):
    rows, columns = terms.shape
    received = exchange(terms.astype(jnp.bfloat16).reshape(size, rows // size, columns), axis)
    return jnp.sum(received.astype(jnp.float32), axis=0)


def collect(block, axis, size):
    return exchange(jnp.broadcast_to(block[None], (size,) + block.shape), axis)


def group_sum(terms, base):
    rows, columns = terms.shape
    pair = sum_over(terms, "core", CORES).astype(jnp.bfloat16)
    return base + jnp.sum(collect(pair, "y", YS).astype(jnp.float32), axis=0)


def lane_squares(values, lanes):
    squares = values * values
    return sum(squares[:, at : at + lanes] for at in range(0, values.shape[1], lanes))


def attend(queries, kv_cache, lengths, fresh_keys, fresh_values, score_scale):
    rows, steps, heads, head_dim = queries.shape
    merged = queries.reshape(rows, steps * heads, head_dim)
    scores = (
        jnp.einsum("rgd,rld->rgl", merged, kv_cache[..., :head_dim], preferred_element_type=jnp.float32)
        * score_scale
    )
    live = jnp.arange(kv_cache.shape[1])[None, None, :] < lengths[:, None, None]
    scores = jnp.where(live, scores, masked_score)
    fresh_scores = (
        jnp.einsum("rgd,rtd->rgt", merged, fresh_keys, preferred_element_type=jnp.float32) * score_scale
    )
    query_step = jnp.arange(steps * heads) // heads
    seen = jnp.arange(steps)[None, None, :] <= query_step[None, :, None]
    fresh_scores = jnp.where(seen, fresh_scores, masked_score)
    highest = jnp.maximum(jnp.max(scores, axis=-1), jnp.max(fresh_scores, axis=-1))[..., None]
    cache_weights = jnp.exp(scores - highest)
    fresh_weights = jnp.exp(fresh_scores - highest)
    total = jnp.sum(cache_weights, axis=-1, keepdims=True) + jnp.sum(
        fresh_weights, axis=-1, keepdims=True
    )
    cache_probs = (cache_weights / total).astype(jnp.bfloat16)
    fresh_probs = (fresh_weights / total).astype(jnp.bfloat16)
    mixed = jnp.einsum(
        "rgl,rld->rgd", cache_probs, kv_cache[..., head_dim:], preferred_element_type=jnp.float32
    ) + jnp.einsum("rgt,rtd->rgd", fresh_probs, fresh_values, preferred_element_type=jnp.float32)
    return mixed.reshape(rows, steps, heads, head_dim)


def body(
    inputs,
    attn_gain,
    w_query,
    w_keyval,
    w_out,
    ffn_gain,
    w_gateup,
    w_down,
    kv_cache,
    lengths,
    positions,
):
    steps, all_rows, local_width = inputs.shape
    local_rows = kv_cache.shape[0]
    head_dim = kv_cache.shape[3] // 2
    local_queries = w_query.shape[1] // head_dim
    local_hidden = w_down.shape[0]
    score_scale = head_dim ** (-0.5)
    keyval_weight = w_keyval.reshape(local_width, 2 * head_dim)
    keyvals_at = local_queries * head_dim
    squares_at = keyvals_at + 2 * head_dim
    rows = steps * all_rows
    x_rows = rows // XS
    half = rows // CORES
    gateup = w_gateup.transpose(1, 2, 0).astype(jnp.float32) * ffn_gain.astype(jnp.float32)
    gateup = gateup.astype(jnp.bfloat16)

    current = (
        inputs.reshape(steps, XS, all_rows // XS, local_width)
        .transpose(1, 0, 2, 3)
        .reshape(rows, local_width)
        .astype(jnp.float32)
    )
    scaled = (current * attn_gain.astype(jnp.float32)).astype(jnp.bfloat16)
    terms = jnp.concatenate(
        [
            jnp.dot(scaled, w_query, preferred_element_type=jnp.float32),
            jnp.dot(scaled, keyval_weight, preferred_element_type=jnp.float32),
            lane_squares(current, 128),
        ],
        axis=1,
    )
    sums = sum_over(terms, "x", XS).astype(jnp.bfloat16)
    sums = sums.reshape(steps, ZS, local_rows, -1).transpose(1, 0, 2, 3).reshape(x_rows, -1)
    sums = sum_over(sums, "z", ZS)
    mean = jnp.sum(sums[:, squares_at:], axis=-1, keepdims=True) / D
    sums = (sums[:, :squares_at] * lax.rsqrt(mean + epsilon)).reshape(steps, local_rows, squares_at)
    offsets = positions[None, :] + jnp.arange(steps)[:, None]
    queries = rotate(
        sums[..., :keyvals_at].reshape(steps, local_rows, local_queries, head_dim), offsets[..., None]
    ).astype(jnp.bfloat16)
    keys_new = rotate(sums[..., keyvals_at : keyvals_at + head_dim], offsets).astype(jnp.bfloat16)
    values_new = sums[..., keyvals_at + head_dim :].astype(jnp.bfloat16)
    new_entries = jnp.concatenate([keys_new, values_new], axis=-1)[:, :, None, :]
    mixed = attend(
        queries.transpose(1, 0, 2, 3),
        kv_cache.reshape(local_rows, -1, 2 * head_dim),
        lengths,
        keys_new.transpose(1, 0, 2),
        values_new.transpose(1, 0, 2),
        score_scale,
    )
    heads = mixed.astype(jnp.bfloat16).transpose(1, 0, 2, 3).reshape(steps * local_rows, keyvals_at)

    all_heads = collect(collect(heads, "z", ZS).reshape(x_rows, keyvals_at), "x", XS)
    attn_terms = jnp.dot(
        all_heads.reshape(rows, keyvals_at), w_out, preferred_element_type=jnp.float32
    )
    residual = lax.dynamic_index_in_dim(
        inputs.reshape(steps, CORES, all_rows // CORES // local_rows, local_rows, local_width),
        lax.axis_index("core"), 1, keepdims=False,
    )
    residual = residual.transpose(1, 0, 2, 3).reshape(half, local_width).astype(jnp.float32)
    state = group_sum(attn_terms, residual)
    ffn_in = lax.all_gather(state.astype(jnp.bfloat16), "core", axis=0, tiled=True)
    squares = ffn_in.astype(jnp.float32)
    squares = squares * squares
    halves = []
    for part in range(2):
        halves.append(
            lax.dot_general(
                ffn_in, gateup[part], (((1,), (1,)), ((), ())), preferred_element_type=jnp.float32
            )
        )
        lanes = squares[:, 128 * part : 128 * part + 128]
        halves.append(lanes[:, :64] + lanes[:, 64:])
    terms = jnp.concatenate(halves, axis=1)
    sums = sum_over(sum_over(terms, "x", XS), "z", ZS)
    padded = local_hidden + 64
    gate, up = sums[:, :padded], sums[:, padded:]
    mean = jnp.sum(gate[:, local_hidden:] + up[:, local_hidden:], axis=-1, keepdims=True) / D
    scale = lax.rsqrt(mean + epsilon)
    activated = jax.nn.silu(gate[:, :local_hidden] * scale) * (up[:, :local_hidden] * scale)
    hidden = collect(activated.astype(jnp.bfloat16), "z", ZS).reshape(x_rows, local_hidden)
    hidden = collect(hidden, "x", XS).reshape(rows, local_hidden)
    down_terms = jnp.dot(hidden, w_down, preferred_element_type=jnp.float32)
    result = group_sum(down_terms, state).astype(jnp.bfloat16)
    result = lax.all_gather(result, "core", axis=0, tiled=True)
    outputs = (
        result.reshape(XS * ZS, steps, local_rows, local_width)
        .transpose(1, 0, 2, 3)
        .reshape(steps, all_rows, local_width)
    )
    return (outputs, new_entries)


def solution(mesh):
    fine = Mesh(mesh.devices.reshape(XS, ZS, YS, CORES), ("x", "z", "y", "core"))
    in_specs = (
        P(None, None, WIDE),
        P(WIDE),
        P(WIDE, MP),
        P(WIDE, MP, None),
        P(MP, WIDE),
        P(WIDE),
        P(WIDE, None, MP),
        P(MP, WIDE),
        P(WIDE, None, MP, None),
        P(WIDE),
        P(WIDE),
    )
    out_specs = (P(None, None, WIDE), P(None, WIDE, MP, None))
    return jax.shard_map(body, mesh=fine, in_specs=in_specs, out_specs=out_specs, check_vma=False)
```

```python
import jax
import jax.numpy as jnp
from jax import lax
from jax.experimental import pallas as pl
from jax.experimental.pallas import tpu as pltpu
from jax.sharding import Mesh, PartitionSpec as P

D = 16384
STEPS = 2

epsilon = 1e-05
rope_base = 500000.0
masked_score = -1e30

WIDE = ("x", "z")
MP = ("y", "core")
XS, ZS, YS, CORES = 4, 16, 4, 2


def rotate(vectors, offsets):
    half_size = vectors.shape[-1] // 2
    freqs = rope_base ** (-(jnp.arange(half_size, dtype=jnp.float32) * 2.0 / vectors.shape[-1]))
    angles = offsets.astype(jnp.float32)[..., None] * freqs
    cosine = jnp.cos(angles)
    sine = jnp.sin(angles)
    first_half = vectors[..., :half_size]
    second_half = vectors[..., half_size:]
    return jnp.concatenate(
        [first_half * cosine - second_half * sine, second_half * cosine + first_half * sine],
        axis=-1,
    )


def exchange(blocks, axis):
    return lax.all_to_all(blocks, axis, 0, 0, tiled=True)


def sum_over(terms, axis, size):
    rows, columns = terms.shape
    received = exchange(terms.astype(jnp.bfloat16).reshape(size, rows // size, columns), axis)
    return jnp.sum(received.astype(jnp.float32), axis=0)


def collect(block, axis, size):
    return exchange(jnp.broadcast_to(block[None], (size,) + block.shape), axis)


def group_terms(terms):
    total = jnp.sum(collect(terms.astype(jnp.bfloat16), "y", YS).astype(jnp.float32), axis=0)
    return lax.all_gather(total.astype(jnp.bfloat16), "core", axis=0, tiled=False)


def to_row_order(count, back):
    dims = (count, count)
    mixed = lax.broadcasted_iota(jnp.int32, dims, 1 if back else 0)
    plain = lax.broadcasted_iota(jnp.int32, dims, 0 if back else 1)
    source = (mixed >> 2) * 2 + (mixed & 1) + ((mixed >> 1) & 1) * (count // 2)
    return jnp.where(source == plain, 1.0, 0.0).astype(jnp.bfloat16)


def first_kernel(inputs_ref, gain_ref, query_ref, keyval_ref, terms_ref, rows_ref):
    group = inputs_ref.shape[1] // XS
    order = to_row_order(2 * group, False)
    gain = gain_ref[...].astype(jnp.float32)
    queries = query_ref.shape[1]
    keyvals = keyval_ref.shape[1]
    scaled = []
    for at in range(XS):
        block = jnp.concatenate([inputs_ref[step, group * at : group * (at + 1)] for step in range(2)], axis=0)
        values = jnp.dot(order, block, preferred_element_type=jnp.float32)
        rows_ref[2 * group * at : 2 * group * (at + 1)] = values.astype(jnp.bfloat16)
        squares = values * values
        terms_ref[at, :, queries + keyvals :] = (squares[:, :128] + squares[:, 128:]).astype(jnp.bfloat16)
        scaled.append((values * gain).astype(jnp.bfloat16))
    scaled = jnp.concatenate(scaled, axis=0)
    for weights_ref, base in ((query_ref, 0), (keyval_ref, queries)):
        for start in range(0, weights_ref.shape[1], 256):
            product = jnp.dot(scaled, weights_ref[:, start : start + 256], preferred_element_type=jnp.float32)
            product = product.astype(jnp.bfloat16).reshape(XS, 2 * group, 256)
            terms_ref[:, :, base + start : base + start + 256] = product


def first_terms(inputs, gain, w_query, w_keyval):
    steps, all_rows, width = inputs.shape
    columns = w_query.shape[1] + w_keyval.shape[1] + 128
    return pl.pallas_call(
        first_kernel,
        out_shape=(
            jax.ShapeDtypeStruct((XS, steps * all_rows // XS, columns), jnp.bfloat16),
            jax.ShapeDtypeStruct((steps * all_rows, width), jnp.bfloat16),
        ),
        compiler_params=pltpu.CompilerParams(vmem_limit_bytes=24 * 1024 * 1024),
        name="first_terms",
    )(inputs, gain.reshape(1, width), w_query, w_keyval)


def gateup_kernel(pair_ref, rows_ref, weights_ref, terms_ref, state_ref):
    state = (
        pair_ref[0].astype(jnp.float32) + pair_ref[1].astype(jnp.float32) + rows_ref[...].astype(jnp.float32)
    )
    state_ref[...] = state
    squares = state * state
    squares = squares[:, :128] + squares[:, 128:]
    hidden = weights_ref.shape[0]
    terms_ref[:, :, hidden:] = squares.astype(jnp.bfloat16).reshape(XS, -1, 128)
    state = state.astype(jnp.bfloat16)
    for start in range(0, hidden, 128):
        product = lax.dot_general(
            state,
            weights_ref[start : start + 128],
            (((1,), (1,)), ((), ())),
            preferred_element_type=jnp.float32,
        )
        terms_ref[:, :, start : start + 128] = product.astype(jnp.bfloat16).reshape(XS, -1, 128)


def gateup_terms(pair, rows, weights):
    count, width = rows.shape
    return pl.pallas_call(
        gateup_kernel,
        out_shape=(
            jax.ShapeDtypeStruct((XS, count // XS, weights.shape[0] + 128), jnp.bfloat16),
            jax.ShapeDtypeStruct((count, width), jnp.float32),
        ),
        compiler_params=pltpu.CompilerParams(vmem_limit_bytes=24 * 1024 * 1024),
        name="gateup_terms",
    )(pair, rows, weights)


def last_kernel(pair_ref, state_ref, outputs_ref):
    group = outputs_ref.shape[1] // XS
    order = to_row_order(2 * group, True)
    for at in range(XS):
        here = slice(2 * group * at, 2 * group * (at + 1))
        values = (
            pair_ref[0, here].astype(jnp.float32) + pair_ref[1, here].astype(jnp.float32) + state_ref[here]
        )
        values = jnp.dot(order, values.astype(jnp.bfloat16), preferred_element_type=jnp.float32)
        values = values.astype(jnp.bfloat16)
        for step in range(2):
            outputs_ref[step, group * at : group * (at + 1)] = values[group * step : group * (step + 1)]


def last_sum(pair, state, steps):
    count, width = state.shape
    return pl.pallas_call(
        last_kernel,
        out_shape=jax.ShapeDtypeStruct((steps, count // steps, width), jnp.bfloat16),
        name="last_sum",
    )(pair, state)


def attend(queries, kv_cache, lengths, fresh_keys, fresh_values, score_scale):
    rows, steps, heads, head_dim = queries.shape
    merged = queries.reshape(rows, steps * heads, head_dim)
    scores = (
        jnp.einsum("rgd,rld->rgl", merged, kv_cache[..., :head_dim], preferred_element_type=jnp.float32)
        * score_scale
    )
    live = jnp.arange(kv_cache.shape[1])[None, None, :] < lengths[:, None, None]
    scores = jnp.where(live, scores, masked_score)
    fresh_scores = (
        jnp.einsum("rgd,rtd->rgt", merged, fresh_keys, preferred_element_type=jnp.float32) * score_scale
    )
    query_step = jnp.arange(steps * heads) // heads
    seen = jnp.arange(steps)[None, None, :] <= query_step[None, :, None]
    fresh_scores = jnp.where(seen, fresh_scores, masked_score)
    highest = jnp.maximum(jnp.max(scores, axis=-1), jnp.max(fresh_scores, axis=-1))[..., None]
    cache_weights = jnp.exp(scores - highest)
    fresh_weights = jnp.exp(fresh_scores - highest)
    total = jnp.sum(cache_weights, axis=-1, keepdims=True) + jnp.sum(
        fresh_weights, axis=-1, keepdims=True
    )
    cache_probs = (cache_weights / total).astype(jnp.bfloat16)
    fresh_probs = (fresh_weights / total).astype(jnp.bfloat16)
    mixed = jnp.einsum(
        "rgl,rld->rgd", cache_probs, kv_cache[..., head_dim:], preferred_element_type=jnp.float32
    ) + jnp.einsum("rgt,rtd->rgd", fresh_probs, fresh_values, preferred_element_type=jnp.float32)
    return mixed.reshape(rows, steps, heads, head_dim)


def body(
    inputs,
    attn_gain,
    w_query,
    w_keyval,
    w_out,
    ffn_gain,
    w_gateup,
    w_down,
    kv_cache,
    lengths,
    positions,
):
    steps, all_rows, local_width = inputs.shape
    local_rows = kv_cache.shape[0]
    head_dim = kv_cache.shape[3] // 2
    local_queries = w_query.shape[1] // head_dim
    local_hidden = w_down.shape[0]
    score_scale = head_dim ** (-0.5)
    keyval_weight = w_keyval.reshape(local_width, 2 * head_dim)
    keyvals_at = local_queries * head_dim
    squares_at = keyvals_at + 2 * head_dim
    rows = steps * all_rows
    x_rows = rows // XS
    gateup = w_gateup.transpose(1, 2, 0).astype(jnp.float32) * ffn_gain.astype(jnp.float32)
    gateup = gateup.astype(jnp.bfloat16).reshape(2 * local_hidden, local_width)

    terms, input_rows = first_terms(inputs, attn_gain, w_query, keyval_weight)
    sums = jnp.sum(exchange(terms, "x").astype(jnp.float32), axis=0)
    sums = sum_over(sums, "z", ZS)
    mean = jnp.sum(sums[:, squares_at:], axis=-1, keepdims=True) / D
    sums = (sums[:, :squares_at] * lax.rsqrt(mean + epsilon)).reshape(steps, local_rows, squares_at)
    offsets = positions[None, :] + jnp.arange(steps)[:, None]
    queries = rotate(
        sums[..., :keyvals_at].reshape(steps, local_rows, local_queries, head_dim), offsets[..., None]
    ).astype(jnp.bfloat16)
    keys_new = rotate(sums[..., keyvals_at : keyvals_at + head_dim], offsets).astype(jnp.bfloat16)
    values_new = sums[..., keyvals_at + head_dim :].astype(jnp.bfloat16)
    new_entries = jnp.concatenate([keys_new, values_new], axis=-1)[:, :, None, :]
    mixed = attend(
        queries.transpose(1, 0, 2, 3),
        kv_cache.reshape(local_rows, -1, 2 * head_dim),
        lengths,
        keys_new.transpose(1, 0, 2),
        values_new.transpose(1, 0, 2),
        score_scale,
    )
    heads = mixed.astype(jnp.bfloat16).transpose(1, 0, 2, 3).reshape(steps * local_rows, keyvals_at)

    all_heads = collect(collect(heads, "z", ZS).reshape(x_rows, keyvals_at), "x", XS)
    attn_terms = jnp.dot(
        all_heads.reshape(rows, keyvals_at), w_out, preferred_element_type=jnp.float32
    )
    terms, state = gateup_terms(group_terms(attn_terms), input_rows, gateup)
    sums = jnp.sum(exchange(terms, "x").astype(jnp.float32), axis=0)
    sums = sum_over(sums, "z", ZS)
    mean = jnp.sum(sums[:, 2 * local_hidden :], axis=-1, keepdims=True) / D
    sums = sums[:, : 2 * local_hidden] * lax.rsqrt(mean + epsilon)
    activated = jax.nn.silu(sums[:, :local_hidden]) * sums[:, local_hidden:]
    hidden = collect(activated.astype(jnp.bfloat16), "z", ZS).reshape(x_rows, local_hidden)
    hidden = collect(hidden, "x", XS).reshape(rows, local_hidden)
    down_terms = jnp.dot(hidden, w_down, preferred_element_type=jnp.float32)
    outputs = last_sum(group_terms(down_terms), state, steps)
    return (outputs, new_entries)


def solution(mesh):
    fine = Mesh(mesh.devices.reshape(XS, ZS, YS, CORES), ("x", "z", "y", "core"))
    in_specs = (
        P(None, None, WIDE),
        P(WIDE),
        P(WIDE, MP),
        P(WIDE, MP, None),
        P(MP, WIDE),
        P(WIDE),
        P(WIDE, None, MP),
        P(MP, WIDE),
        P(WIDE, None, MP, None),
        P(WIDE),
        P(WIDE),
    )
    out_specs = (P(None, None, WIDE), P(None, WIDE, MP, None))
    return jax.shard_map(body, mesh=fine, in_specs=in_specs, out_specs=out_specs, check_vma=False)
```

```python
import functools

import jax
import jax.numpy as jnp
from jax import lax
from jax.experimental import pallas as pl
from jax.experimental.pallas import tpu as pltpu
from jax.sharding import Mesh, PartitionSpec as P

D = 16384
STEPS = 2

epsilon = 1e-05
rope_base = 500000.0
masked_score = -1e30

WIDE = ("x", "z")
MP = ("y", "core")
XS, ZS, YS, CORES = 4, 16, 4, 2
EARLY = 896
EARLY_CUT, LATE_CUT, DOWN_CUT = 512, 384, 384


def rotate(vectors, offsets):
    half_size = vectors.shape[-1] // 2
    freqs = rope_base ** (-(jnp.arange(half_size, dtype=jnp.float32) * 2.0 / vectors.shape[-1]))
    angles = offsets.astype(jnp.float32)[..., None] * freqs
    cosine = jnp.cos(angles)
    sine = jnp.sin(angles)
    first_half = vectors[..., :half_size]
    second_half = vectors[..., half_size:]
    return jnp.concatenate(
        [first_half * cosine - second_half * sine, second_half * cosine + first_half * sine],
        axis=-1,
    )


def exchange(blocks, axis):
    return lax.all_to_all(blocks, axis, 0, 0, tiled=True)


def sum_over(terms, axis, size):
    rows, columns = terms.shape
    received = exchange(terms.astype(jnp.bfloat16).reshape(size, rows // size, columns), axis)
    return jnp.sum(received.astype(jnp.float32), axis=0)


def collect(block, axis, size):
    return exchange(jnp.broadcast_to(block[None], (size,) + block.shape), axis)


def group_terms(blocks):
    shape = blocks.shape
    copies = jnp.broadcast_to(blocks[:, None], (XS, YS) + shape[1:])
    return exchange(copies.reshape((XS * YS,) + shape[1:]), ("x", "y"))


def pair_terms(received):
    blocks = received.reshape((XS, YS) + received.shape[1:])
    total = jnp.sum(blocks.astype(jnp.float32), axis=1)
    return lax.all_gather(total.astype(jnp.bfloat16), "core", axis=0, tiled=False)


def shift(block, by):
    return lax.ppermute(block, "x", [(at, (at + by) % XS) for at in range(XS)])


def both_ways(block):
    return shift(block, -1), shift(block, 1)


def far_block(after, before, cut):
    return shift(before[:cut], 1), shift(after[cut:], -1)


def together(*values):
    return lax.optimization_barrier(values)


def to_row_order(count, back):
    dims = (count, count)
    mixed = lax.broadcasted_iota(jnp.int32, dims, 1 if back else 0)
    plain = lax.broadcasted_iota(jnp.int32, dims, 0 if back else 1)
    source = (mixed >> 2) * 2 + (mixed & 1) + ((mixed >> 1) & 1) * (count // 2)
    return jnp.where(source == plain, 1.0, 0.0).astype(jnp.bfloat16)


def first_kernel(inputs_ref, gain_ref, query_ref, keyval_ref, terms_ref, rows_ref):
    group = inputs_ref.shape[1] // XS
    order = to_row_order(2 * group, False)
    gain = gain_ref[...].astype(jnp.float32)
    queries = query_ref.shape[1]
    keyvals = keyval_ref.shape[1]
    scaled = []
    for at in range(XS):
        block = jnp.concatenate([inputs_ref[step, group * at : group * (at + 1)] for step in range(2)], axis=0)
        values = jnp.dot(order, block, preferred_element_type=jnp.float32)
        rows_ref[2 * group * at : 2 * group * (at + 1)] = values.astype(jnp.bfloat16)
        squares = values * values
        terms_ref[at, :, queries + keyvals :] = (squares[:, :128] + squares[:, 128:]).astype(jnp.bfloat16)
        scaled.append((values * gain).astype(jnp.bfloat16))
    scaled = jnp.concatenate(scaled, axis=0)
    for weights_ref, base in ((query_ref, 0), (keyval_ref, queries)):
        for start in range(0, weights_ref.shape[1], 256):
            product = jnp.dot(scaled, weights_ref[:, start : start + 256], preferred_element_type=jnp.float32)
            product = product.astype(jnp.bfloat16).reshape(XS, 2 * group, 256)
            terms_ref[:, :, base + start : base + start + 256] = product


def first_terms(inputs, gain, w_query, w_keyval):
    steps, all_rows, width = inputs.shape
    columns = w_query.shape[1] + w_keyval.shape[1] + 128
    return pl.pallas_call(
        first_kernel,
        out_shape=(
            jax.ShapeDtypeStruct((XS, steps * all_rows // XS, columns), jnp.bfloat16),
            jax.ShapeDtypeStruct((steps * all_rows, width), jnp.bfloat16),
        ),
        compiler_params=pltpu.CompilerParams(vmem_limit_bytes=56 * 1024 * 1024),
        name="first_terms",
    )(inputs, gain.reshape(1, width), w_query, w_keyval)


def gateup_kernel(cuts, at_ref, pair_ref, *refs):
    pieces, (terms_ref, state_ref) = refs[:-2], refs[-2:]
    total = 0.0
    states = []
    for step in range(XS):
        block = (at_ref[0] + step) & (XS - 1)
        state = pair_ref[0, block].astype(jnp.float32) + pair_ref[1, block].astype(jnp.float32)
        state_ref[step] = state
        total += state * state
        states.append(state.astype(jnp.bfloat16))
    hidden = terms_ref.shape[1] - 128
    terms_ref[:, hidden:] = (total[:, :128] + total[:, 128:]).astype(jnp.bfloat16)
    for start in range(0, hidden, 128):
        product = 0.0
        for (step, base), piece_ref in zip(cuts, pieces):
            if base <= start < base + piece_ref.shape[0]:
                product += lax.dot_general(
                    states[step],
                    piece_ref[start - base : start - base + 128],
                    (((1,), (1,)), ((), ())),
                    preferred_element_type=jnp.float32,
                )
        terms_ref[:, start : start + 128] = product.astype(jnp.bfloat16)


def in_vmem(count):
    return [pl.BlockSpec(memory_space=pltpu.VMEM)] * count


def gateup_terms(at, pair, hidden, cuts, pieces):
    _, blocks, count, width = pair.shape
    return pl.pallas_call(
        functools.partial(gateup_kernel, cuts),
        out_shape=(
            jax.ShapeDtypeStruct((count, hidden + 128), jnp.bfloat16),
            jax.ShapeDtypeStruct((blocks, count, width), jnp.float32),
        ),
        in_specs=[pl.BlockSpec(memory_space=pltpu.SMEM)] + in_vmem(1 + len(pieces)),
        compiler_params=pltpu.CompilerParams(vmem_limit_bytes=24 * 1024 * 1024),
        name="gateup_terms",
    )(at, pair, *pieces)


def down_kernel(cuts, at_ref, hidden_ref, state_ref, *refs):
    pieces, terms_ref = refs[:-1], refs[-1]
    for step in range(XS):
        product = state_ref[step] * (1.0 / (YS * CORES))
        for (owner, base), piece_ref in zip(cuts, pieces):
            if owner == step:
                product += jnp.dot(
                    hidden_ref[:, base : base + piece_ref.shape[0]],
                    piece_ref[...],
                    preferred_element_type=jnp.float32,
                )
        terms_ref[(at_ref[0] + step) & (XS - 1)] = product.astype(jnp.bfloat16)


def down_terms(at, hidden, state, cuts, pieces):
    return pl.pallas_call(
        functools.partial(down_kernel, cuts),
        out_shape=jax.ShapeDtypeStruct(state.shape, jnp.bfloat16),
        in_specs=[pl.BlockSpec(memory_space=pltpu.SMEM)] + in_vmem(2 + len(pieces)),
        compiler_params=pltpu.CompilerParams(vmem_limit_bytes=24 * 1024 * 1024),
        name="down_terms",
    )(at, hidden, state, *pieces)


def last_kernel(pair_ref, outputs_ref):
    group = outputs_ref.shape[1] // XS
    order = to_row_order(2 * group, True)
    for at in range(XS):
        values = pair_ref[0, at].astype(jnp.float32) + pair_ref[1, at].astype(jnp.float32)
        values = jnp.dot(order, values.astype(jnp.bfloat16), preferred_element_type=jnp.float32)
        values = values.astype(jnp.bfloat16)
        for step in range(2):
            outputs_ref[step, group * at : group * (at + 1)] = values[group * step : group * (step + 1)]


def last_sum(pair, steps):
    _, blocks, count, width = pair.shape
    return pl.pallas_call(
        last_kernel,
        out_shape=jax.ShapeDtypeStruct((steps, blocks * count // steps, width), jnp.bfloat16),
        name="last_sum",
    )(pair)


def attend(queries, kv_cache, lengths, fresh_keys, fresh_values, score_scale):
    rows, steps, heads, head_dim = queries.shape
    merged = queries.reshape(rows, steps * heads, head_dim)
    scores = (
        jnp.einsum("rgd,rld->rgl", merged, kv_cache[..., :head_dim], preferred_element_type=jnp.float32)
        * score_scale
    )
    live = jnp.arange(kv_cache.shape[1])[None, None, :] < lengths[:, None, None]
    scores = jnp.where(live, scores, masked_score)
    fresh_scores = (
        jnp.einsum("rgd,rtd->rgt", merged, fresh_keys, preferred_element_type=jnp.float32) * score_scale
    )
    query_step = jnp.arange(steps * heads) // heads
    seen = jnp.arange(steps)[None, None, :] <= query_step[None, :, None]
    fresh_scores = jnp.where(seen, fresh_scores, masked_score)
    highest = jnp.maximum(jnp.max(scores, axis=-1), jnp.max(fresh_scores, axis=-1))[..., None]
    cache_weights = jnp.exp(scores - highest)
    fresh_weights = jnp.exp(fresh_scores - highest)
    total = jnp.sum(cache_weights, axis=-1, keepdims=True) + jnp.sum(
        fresh_weights, axis=-1, keepdims=True
    )
    cache_probs = (cache_weights / total).astype(jnp.bfloat16)
    fresh_probs = (fresh_weights / total).astype(jnp.bfloat16)
    mixed = jnp.einsum(
        "rgl,rld->rgd", cache_probs, kv_cache[..., head_dim:], preferred_element_type=jnp.float32
    ) + jnp.einsum("rgt,rtd->rgd", fresh_probs, fresh_values, preferred_element_type=jnp.float32)
    return mixed.reshape(rows, steps, heads, head_dim)


def body(
    inputs,
    attn_gain,
    w_query,
    w_keyval,
    w_out,
    ffn_gain,
    w_gateup,
    w_down,
    kv_cache,
    lengths,
    positions,
):
    steps, all_rows, local_width = inputs.shape
    local_rows = kv_cache.shape[0]
    head_dim = kv_cache.shape[3] // 2
    local_queries = w_query.shape[1] // head_dim
    local_hidden = w_down.shape[0]
    score_scale = head_dim ** (-0.5)
    keyval_weight = w_keyval.reshape(local_width, 2 * head_dim)
    keyvals_at = local_queries * head_dim
    squares_at = keyvals_at + 2 * head_dim
    rows = steps * all_rows
    x_rows = rows // XS
    gateup = w_gateup.transpose(1, 2, 0).reshape(2 * local_hidden, local_width)
    gain = ffn_gain.astype(jnp.float32)
    early = (gateup[:EARLY].astype(jnp.float32) * gain).astype(jnp.bfloat16)
    late = (gateup[EARLY:].astype(jnp.float32) * gain).astype(jnp.bfloat16)

    terms, input_rows = first_terms(inputs, attn_gain, w_query, keyval_weight)
    sums = jnp.sum(exchange(terms, "x").astype(jnp.float32), axis=0).astype(jnp.bfloat16)
    sums, early = together(sums, early)
    early_after, early_before = both_ways(early)
    sums = exchange(sums.reshape(ZS, -1, sums.shape[1]), "z")
    sums, early_after, early_before, late = together(sums, early_after, early_before, late)
    early_far = far_block(early_after, early_before, EARLY_CUT)
    late_after, late_before = both_ways(late)
    sums = jnp.sum(sums.astype(jnp.float32), axis=0)
    mean = jnp.sum(sums[:, squares_at:], axis=-1, keepdims=True) / D
    sums = (sums[:, :squares_at] * lax.rsqrt(mean + epsilon)).reshape(steps, local_rows, squares_at)
    offsets = positions[None, :] + jnp.arange(steps)[:, None]
    queries = rotate(
        sums[..., :keyvals_at].reshape(steps, local_rows, local_queries, head_dim), offsets[..., None]
    ).astype(jnp.bfloat16)
    keys_new = rotate(sums[..., keyvals_at : keyvals_at + head_dim], offsets).astype(jnp.bfloat16)
    values_new = sums[..., keyvals_at + head_dim :].astype(jnp.bfloat16)
    new_entries = jnp.concatenate([keys_new, values_new], axis=-1)[:, :, None, :]
    mixed = attend(
        queries.transpose(1, 0, 2, 3),
        kv_cache.reshape(local_rows, -1, 2 * head_dim),
        lengths,
        keys_new.transpose(1, 0, 2),
        values_new.transpose(1, 0, 2),
        score_scale,
    )
    heads = mixed.astype(jnp.bfloat16).transpose(1, 0, 2, 3).reshape(steps * local_rows, keyvals_at)

    all_heads = collect(heads, "z", ZS)
    all_heads, late_after, late_before, *early_far = together(
        all_heads, late_after, late_before, *early_far
    )
    all_heads = collect(all_heads.reshape(x_rows, keyvals_at), "x", XS).reshape(rows, keyvals_at)
    attn_terms = jnp.dot(all_heads, w_out, preferred_element_type=jnp.float32) + (
        input_rows.astype(jnp.float32) * (1.0 / (YS * CORES))
    )
    attn_terms = attn_terms.astype(jnp.bfloat16).reshape(XS, x_rows, local_width)
    attn_terms, late_after, late_before = together(attn_terms, late_after, late_before)
    late_far = far_block(late_after, late_before, LATE_CUT)
    received = group_terms(attn_terms)
    received, *late_far = together(received, *late_far)
    at = lax.axis_index("x")[None]
    cuts = ((0, 0), (0, EARLY), (1, 0), (1, EARLY), (3, 0), (3, EARLY))
    cuts += ((2, 0), (2, EARLY_CUT), (2, EARLY), (2, EARLY + LATE_CUT))
    terms, state = gateup_terms(
        at,
        pair_terms(received),
        2 * local_hidden,
        cuts,
        (early, late, early_after, late_after, early_before, late_before, *early_far, *late_far),
    )
    terms, w_down = together(terms, w_down)
    down_after, down_before = both_ways(w_down)
    sums = exchange(terms.reshape(ZS, -1, terms.shape[1]), "z")
    sums, down_after, down_before = together(sums, down_after, down_before)
    down_far = far_block(down_after, down_before, DOWN_CUT)
    sums = jnp.sum(sums.astype(jnp.float32), axis=0)
    mean = jnp.sum(sums[:, 2 * local_hidden :], axis=-1, keepdims=True) / D
    sums = sums[:, : 2 * local_hidden] * lax.rsqrt(mean + epsilon)
    activated = jax.nn.silu(sums[:, :local_hidden]) * sums[:, local_hidden:]
    hidden = collect(activated.astype(jnp.bfloat16), "z", ZS)
    hidden, *down_far = together(hidden, *down_far)
    blocks = down_terms(
        at,
        hidden.reshape(x_rows, local_hidden),
        state,
        ((0, 0), (1, 0), (3, 0), (2, 0), (2, DOWN_CUT)),
        (w_down, down_after, down_before, *down_far),
    )
    outputs = last_sum(pair_terms(group_terms(blocks)), steps)
    return (outputs, new_entries)


def solution(mesh):
    fine = Mesh(mesh.devices.reshape(XS, ZS, YS, CORES), ("x", "z", "y", "core"))
    in_specs = (
        P(None, None, WIDE),
        P(WIDE),
        P(WIDE, MP),
        P(WIDE, MP, None),
        P(MP, WIDE),
        P(WIDE),
        P(WIDE, None, MP),
        P(MP, WIDE),
        P(WIDE, None, MP, None),
        P(WIDE),
        P(WIDE),
    )
    out_specs = (P(None, None, WIDE), P(None, WIDE, MP, None))
    return jax.shard_map(body, mesh=fine, in_specs=in_specs, out_specs=out_specs, check_vma=False)
```

```python
import jax
import jax.numpy as jnp
from jax import lax
from jax.experimental import pallas as pl
from jax.experimental.pallas import tpu as pltpu
from jax.sharding import Mesh, PartitionSpec as P

D = 16384
STEPS = 2

epsilon = 1e-05
rope_base = 500000.0
masked_score = -1e30

WIDE = ("x", "z")
MP = ("y", "core")
XS, ZS, YS, CORES = 4, 16, 4, 2
QUERY_CHUNKS = 4


def rotate(vectors, offsets):
    half_size = vectors.shape[-1] // 2
    freqs = rope_base ** (-(jnp.arange(half_size, dtype=jnp.float32) * 2.0 / vectors.shape[-1]))
    angles = offsets.astype(jnp.float32)[..., None] * freqs
    cosine = jnp.cos(angles)
    sine = jnp.sin(angles)
    first_half = vectors[..., :half_size]
    second_half = vectors[..., half_size:]
    return jnp.concatenate(
        [first_half * cosine - second_half * sine, second_half * cosine + first_half * sine],
        axis=-1,
    )


def exchange(blocks, axis):
    return lax.all_to_all(blocks, axis, 0, 0, tiled=True)


def sum_over(terms, axis, size):
    rows, columns = terms.shape
    received = exchange(terms.astype(jnp.bfloat16).reshape(size, rows // size, columns), axis)
    return jnp.sum(received.astype(jnp.float32), axis=0)


def collect(block, axis, size):
    return exchange(jnp.broadcast_to(block[None], (size,) + block.shape), axis)


def group_terms(copies):
    total = jnp.sum(exchange(copies, "y").astype(jnp.float32), axis=0)
    return lax.all_gather(total.astype(jnp.bfloat16), "core", axis=0, tiled=False)


def to_row_order(count):
    dims = (count, count)
    mixed = lax.broadcasted_iota(jnp.int32, dims, 0)
    plain = lax.broadcasted_iota(jnp.int32, dims, 1)
    source = (mixed >> 2) * 2 + (mixed & 1) + ((mixed >> 1) & 1) * (count // 2)
    return jnp.where(source == plain, 1.0, 0.0).astype(jnp.bfloat16)


def first_kernel(
    inputs_hbm, gain_ref, query_hbm, keyval_hbm, terms_ref, rows_ref, inputs_ref, query_ref, keyval_ref, sems
):
    group = inputs_ref.shape[1] // XS
    queries = query_ref.shape[1]
    keyvals = keyval_ref.shape[1]
    chunk = queries // QUERY_CHUNKS
    copies = [pltpu.make_async_copy(inputs_hbm, inputs_ref, sems.at[0])]
    for at in range(QUERY_CHUNKS):
        here = slice(chunk * at, chunk * (at + 1))
        copies.append(pltpu.make_async_copy(query_hbm.at[:, here], query_ref.at[:, here], sems.at[1 + at]))
    copies.append(pltpu.make_async_copy(keyval_hbm, keyval_ref, sems.at[1 + QUERY_CHUNKS]))
    for copy in copies:
        copy.start()
    order = to_row_order(2 * group)
    gain = gain_ref[...].astype(jnp.float32)
    copies[0].wait()
    scaled = []
    for at in range(XS):
        block = jnp.concatenate([inputs_ref[step, group * at : group * (at + 1)] for step in range(2)], axis=0)
        values = jnp.dot(order, block, preferred_element_type=jnp.float32)
        rows_ref[2 * group * at : 2 * group * (at + 1)] = values.astype(jnp.bfloat16)
        squares = values * values
        terms_ref[at, :, queries + keyvals :] = (squares[:, :128] + squares[:, 128:]).astype(jnp.bfloat16)
        scaled.append((values * gain).astype(jnp.bfloat16))
    scaled = jnp.concatenate(scaled, axis=0)
    for at in range(QUERY_CHUNKS + 1):
        copies[1 + at].wait()
        last = at == QUERY_CHUNKS
        weights_ref, base = (keyval_ref, queries) if last else (query_ref, 0)
        for start in range(0, keyvals, 256) if last else range(chunk * at, chunk * (at + 1), 256):
            product = jnp.dot(scaled, weights_ref[:, start : start + 256], preferred_element_type=jnp.float32)
            product = product.astype(jnp.bfloat16).reshape(XS, 2 * group, 256)
            terms_ref[:, :, base + start : base + start + 256] = product


def first_terms(inputs, gain, w_query, w_keyval):
    steps, all_rows, width = inputs.shape
    columns = w_query.shape[1] + w_keyval.shape[1] + 128
    anywhere = pl.BlockSpec(memory_space=pl.ANY)
    return pl.pallas_call(
        first_kernel,
        out_shape=(
            jax.ShapeDtypeStruct((XS, steps * all_rows // XS, columns), jnp.bfloat16),
            jax.ShapeDtypeStruct((steps * all_rows, width), jnp.bfloat16),
        ),
        in_specs=[anywhere, pl.BlockSpec(memory_space=pltpu.VMEM), anywhere, anywhere],
        scratch_shapes=[
            pltpu.VMEM(inputs.shape, jnp.bfloat16),
            pltpu.VMEM(w_query.shape, jnp.bfloat16),
            pltpu.VMEM(w_keyval.shape, jnp.bfloat16),
            pltpu.SemaphoreType.DMA((QUERY_CHUNKS + 2,)),
        ],
        compiler_params=pltpu.CompilerParams(vmem_limit_bytes=56 * 1024 * 1024),
        name="first_terms",
    )(inputs, gain.reshape(1, width), w_query, w_keyval)


def spread_kernel(rows_ref, weights_ref, copies_ref):
    product = jnp.dot(rows_ref[...], weights_ref[...], preferred_element_type=jnp.float32)
    product = product.astype(jnp.bfloat16)
    for at in range(copies_ref.shape[0]):
        copies_ref[at] = product


def spread_dot(rows, weights, copies):
    return pl.pallas_call(
        spread_kernel,
        out_shape=jax.ShapeDtypeStruct((copies, rows.shape[0], weights.shape[1]), jnp.bfloat16),
        compiler_params=pltpu.CompilerParams(vmem_limit_bytes=24 * 1024 * 1024),
        name="spread_dot",
    )(rows, weights)


def gateup_kernel(pair_ref, rows_ref, weights_ref, terms_ref, state_ref):
    state = (
        pair_ref[0].astype(jnp.float32) + pair_ref[1].astype(jnp.float32) + rows_ref[...].astype(jnp.float32)
    )
    state_ref[...] = state
    squares = state * state
    squares = squares[:, :128] + squares[:, 128:]
    hidden = weights_ref.shape[0]
    terms_ref[:, :, hidden:] = squares.astype(jnp.bfloat16).reshape(XS, -1, 128)
    state = state.astype(jnp.bfloat16)
    for start in range(0, hidden, 128):
        product = lax.dot_general(
            state,
            weights_ref[start : start + 128],
            (((1,), (1,)), ((), ())),
            preferred_element_type=jnp.float32,
        )
        terms_ref[:, :, start : start + 128] = product.astype(jnp.bfloat16).reshape(XS, -1, 128)


def gateup_terms(pair, rows, weights):
    count, width = rows.shape
    return pl.pallas_call(
        gateup_kernel,
        out_shape=(
            jax.ShapeDtypeStruct((XS, count // XS, weights.shape[0] + 128), jnp.bfloat16),
            jax.ShapeDtypeStruct((count, width), jnp.float32),
        ),
        compiler_params=pltpu.CompilerParams(vmem_limit_bytes=24 * 1024 * 1024),
        name="gateup_terms",
    )(pair, rows, weights)


def attend(queries, kv_cache, lengths, fresh_keys, fresh_values, score_scale):
    rows, steps, heads, head_dim = queries.shape
    merged = queries.reshape(rows, steps * heads, head_dim)
    scores = (
        jnp.einsum("rgd,rld->rgl", merged, kv_cache[..., :head_dim], preferred_element_type=jnp.float32)
        * score_scale
    )
    live = jnp.arange(kv_cache.shape[1])[None, None, :] < lengths[:, None, None]
    scores = jnp.where(live, scores, masked_score)
    fresh_scores = (
        jnp.einsum("rgd,rtd->rgt", merged, fresh_keys, preferred_element_type=jnp.float32) * score_scale
    )
    query_step = jnp.arange(steps * heads) // heads
    seen = jnp.arange(steps)[None, None, :] <= query_step[None, :, None]
    fresh_scores = jnp.where(seen, fresh_scores, masked_score)
    highest = jnp.maximum(jnp.max(scores, axis=-1), jnp.max(fresh_scores, axis=-1))[..., None]
    cache_weights = jnp.exp(scores - highest)
    fresh_weights = jnp.exp(fresh_scores - highest)
    total = jnp.sum(cache_weights, axis=-1, keepdims=True) + jnp.sum(
        fresh_weights, axis=-1, keepdims=True
    )
    cache_probs = (cache_weights / total).astype(jnp.bfloat16)
    fresh_probs = (fresh_weights / total).astype(jnp.bfloat16)
    mixed = jnp.einsum(
        "rgl,rld->rgd", cache_probs, kv_cache[..., head_dim:], preferred_element_type=jnp.float32
    ) + jnp.einsum("rgt,rtd->rgd", fresh_probs, fresh_values, preferred_element_type=jnp.float32)
    return mixed.reshape(rows, steps, heads, head_dim)


def body(
    inputs,
    attn_gain,
    w_query,
    w_keyval,
    w_out,
    ffn_gain,
    w_gateup,
    w_down,
    kv_cache,
    lengths,
    positions,
):
    steps, all_rows, local_width = inputs.shape
    local_rows = kv_cache.shape[0]
    head_dim = kv_cache.shape[3] // 2
    local_queries = w_query.shape[1] // head_dim
    local_hidden = w_down.shape[0]
    score_scale = head_dim ** (-0.5)
    keyval_weight = w_keyval.reshape(local_width, 2 * head_dim)
    keyvals_at = local_queries * head_dim
    squares_at = keyvals_at + 2 * head_dim
    rows = steps * all_rows
    x_rows = rows // XS
    gateup = w_gateup.transpose(1, 2, 0).astype(jnp.float32) * ffn_gain.astype(jnp.float32)
    gateup = gateup.astype(jnp.bfloat16).reshape(2 * local_hidden, local_width)

    terms, input_rows = first_terms(inputs, attn_gain, w_query, keyval_weight)
    sums = jnp.sum(exchange(terms, "x").astype(jnp.float32), axis=0)
    sums = sum_over(sums, "z", ZS)
    mean = jnp.sum(sums[:, squares_at:], axis=-1, keepdims=True) / D
    sums = (sums[:, :squares_at] * lax.rsqrt(mean + epsilon)).reshape(steps, local_rows, squares_at)
    offsets = positions[None, :] + jnp.arange(steps)[:, None]
    queries = rotate(
        sums[..., :keyvals_at].reshape(steps, local_rows, local_queries, head_dim), offsets[..., None]
    ).astype(jnp.bfloat16)
    keys_new = rotate(sums[..., keyvals_at : keyvals_at + head_dim], offsets).astype(jnp.bfloat16)
    values_new = sums[..., keyvals_at + head_dim :].astype(jnp.bfloat16)
    new_entries = jnp.concatenate([keys_new, values_new], axis=-1)[:, :, None, :]
    mixed = attend(
        queries.transpose(1, 0, 2, 3),
        kv_cache.reshape(local_rows, -1, 2 * head_dim),
        lengths,
        keys_new.transpose(1, 0, 2),
        values_new.transpose(1, 0, 2),
        score_scale,
    )
    heads = mixed.astype(jnp.bfloat16).transpose(1, 0, 2, 3).reshape(steps * local_rows, keyvals_at)

    all_heads = collect(collect(heads, "z", ZS).reshape(x_rows, keyvals_at), "x", XS)
    pair = group_terms(spread_dot(all_heads.reshape(rows, keyvals_at), w_out, YS))
    terms, state = gateup_terms(pair, input_rows, gateup)
    sums = jnp.sum(exchange(terms, "x").astype(jnp.float32), axis=0)
    sums = sum_over(sums, "z", ZS)
    mean = jnp.sum(sums[:, 2 * local_hidden :], axis=-1, keepdims=True) / D
    sums = sums[:, : 2 * local_hidden] * lax.rsqrt(mean + epsilon)
    activated = jax.nn.silu(sums[:, :local_hidden]) * sums[:, local_hidden:]
    hidden = collect(activated.astype(jnp.bfloat16), "z", ZS).reshape(x_rows, local_hidden)
    hidden = collect(hidden, "x", XS).reshape(rows, local_hidden)
    pair = group_terms(spread_dot(hidden, w_down, YS)).astype(jnp.float32)
    result = (pair[0] + pair[1] + state).astype(jnp.bfloat16)
    outputs = (
        result.reshape(XS * ZS, steps, local_rows, local_width)
        .transpose(1, 0, 2, 3)
        .reshape(steps, all_rows, local_width)
    )
    return (outputs, new_entries)


def solution(mesh):
    fine = Mesh(mesh.devices.reshape(XS, ZS, YS, CORES), ("x", "z", "y", "core"))
    in_specs = (
        P(None, None, WIDE),
        P(WIDE),
        P(WIDE, MP),
        P(WIDE, MP, None),
        P(MP, WIDE),
        P(WIDE),
        P(WIDE, None, MP),
        P(MP, WIDE),
        P(WIDE, None, MP, None),
        P(WIDE),
        P(WIDE),
    )
    out_specs = (P(None, None, WIDE), P(None, WIDE, MP, None))
    return jax.shard_map(body, mesh=fine, in_specs=in_specs, out_specs=out_specs, check_vma=False)
```

```python
import jax
import jax.numpy as jnp
from jax import lax
from jax.experimental import pallas as pl
from jax.experimental.pallas import tpu as pltpu
from jax.sharding import Mesh, PartitionSpec as P

D = 16384
STEPS = 2

epsilon = 1e-05
rope_base = 500000.0
masked_score = -1e30

WIDE = ("x", "z")
MP = ("y", "core")
XS, ZS, YS, CORES = 4, 16, 4, 2
QUERY_CHUNKS = 4


def rotate(vectors, offsets):
    half_size = vectors.shape[-1] // 2
    freqs = rope_base ** (-(jnp.arange(half_size, dtype=jnp.float32) * 2.0 / vectors.shape[-1]))
    angles = offsets.astype(jnp.float32)[..., None] * freqs
    cosine = jnp.cos(angles)
    sine = jnp.sin(angles)
    first_half = vectors[..., :half_size]
    second_half = vectors[..., half_size:]
    return jnp.concatenate(
        [first_half * cosine - second_half * sine, second_half * cosine + first_half * sine],
        axis=-1,
    )


def exchange(blocks, axis):
    return lax.all_to_all(blocks, axis, 0, 0, tiled=True)


def sum_over(terms, axis, size):
    rows, columns = terms.shape
    received = exchange(terms.astype(jnp.bfloat16).reshape(size, rows // size, columns), axis)
    return jnp.sum(received.astype(jnp.float32), axis=0)


def collect(block, axis, size):
    return exchange(jnp.broadcast_to(block[None], (size,) + block.shape), axis)


def group_terms(copies):
    total = jnp.sum(exchange(copies, "y").astype(jnp.float32), axis=0)
    return lax.all_gather(total.astype(jnp.bfloat16), "core", axis=0, tiled=False)


def to_row_order(count):
    dims = (count, count)
    mixed = lax.broadcasted_iota(jnp.int32, dims, 0)
    plain = lax.broadcasted_iota(jnp.int32, dims, 1)
    source = (mixed >> 2) * 2 + (mixed & 1) + ((mixed >> 1) & 1) * (count // 2)
    return jnp.where(source == plain, 1.0, 0.0).astype(jnp.bfloat16)


def first_kernel(
    inputs_hbm, gain_hbm, query_hbm, keyval_hbm, terms_hbm, rows_hbm,
    inputs_ref, gain_ref, query_ref, keyval_ref, terms_ref, rows_ref, sems, out_sems,
):
    group = inputs_ref.shape[1] // XS
    queries = query_ref.shape[1]
    keyvals = keyval_ref.shape[1]
    chunk = queries // QUERY_CHUNKS
    parts = [slice(chunk * at, chunk * (at + 1)) for at in range(QUERY_CHUNKS)]
    copies = [
        pltpu.make_async_copy(inputs_hbm, inputs_ref, sems.at[0]),
        pltpu.make_async_copy(gain_hbm, gain_ref, sems.at[1]),
        pltpu.make_async_copy(keyval_hbm, keyval_ref, sems.at[2]),
    ]
    for at, here in enumerate(parts):
        copies.append(pltpu.make_async_copy(query_hbm.at[:, here], query_ref.at[:, here], sems.at[3 + at]))
    for copy in copies:
        copy.start()
    order = to_row_order(2 * group)
    copies[0].wait()
    copies[1].wait()
    gain = gain_ref[...].astype(jnp.float32)[None]
    scaled = []
    for at in range(XS):
        block = jnp.concatenate([inputs_ref[step, group * at : group * (at + 1)] for step in range(2)], axis=0)
        values = jnp.dot(order, block, preferred_element_type=jnp.float32)
        rows_ref[2 * group * at : 2 * group * (at + 1)] = values.astype(jnp.bfloat16)
        squares = values * values
        terms_ref[at, :, queries + keyvals :] = (squares[:, :128] + squares[:, 128:]).astype(jnp.bfloat16)
        scaled.append((values * gain).astype(jnp.bfloat16))
    scaled = jnp.concatenate(scaled, axis=0)
    results = [pltpu.make_async_copy(rows_ref, rows_hbm, out_sems.at[0])]
    results[0].start()
    copies[2].wait()
    product = jnp.dot(scaled, keyval_ref[...], preferred_element_type=jnp.float32)
    terms_ref[:, :, queries : queries + keyvals] = product.astype(jnp.bfloat16).reshape(XS, 2 * group, keyvals)
    for at, here in enumerate([slice(queries, terms_ref.shape[2])] + parts):
        if at > 0:
            copies[2 + at].wait()
            for start in range(here.start, here.stop, 256):
                product = jnp.dot(scaled, query_ref[:, start : start + 256], preferred_element_type=jnp.float32)
                product = product.astype(jnp.bfloat16).reshape(XS, 2 * group, 256)
                terms_ref[:, :, start : start + 256] = product
        results.append(
            pltpu.make_async_copy(terms_ref.at[:, :, here], terms_hbm.at[:, :, here], out_sems.at[1 + at])
        )
        results[-1].start()
    for result in results:
        result.wait()


def first_terms(inputs, gain, w_query, w_keyval):
    steps, all_rows, width = inputs.shape
    columns = w_query.shape[1] + w_keyval.shape[1] + 128
    anywhere = pl.BlockSpec(memory_space=pl.ANY)
    terms = (XS, steps * all_rows // XS, columns)
    rows = (steps * all_rows, width)
    return pl.pallas_call(
        first_kernel,
        out_shape=(jax.ShapeDtypeStruct(terms, jnp.bfloat16), jax.ShapeDtypeStruct(rows, jnp.bfloat16)),
        in_specs=[anywhere] * 4,
        out_specs=(anywhere, anywhere),
        scratch_shapes=[
            pltpu.VMEM(inputs.shape, jnp.bfloat16),
            pltpu.VMEM(gain.shape, jnp.bfloat16),
            pltpu.VMEM(w_query.shape, jnp.bfloat16),
            pltpu.VMEM(w_keyval.shape, jnp.bfloat16),
            pltpu.VMEM(terms, jnp.bfloat16),
            pltpu.VMEM(rows, jnp.bfloat16),
            pltpu.SemaphoreType.DMA((QUERY_CHUNKS + 3,)),
            pltpu.SemaphoreType.DMA((QUERY_CHUNKS + 2,)),
        ],
        compiler_params=pltpu.CompilerParams(vmem_limit_bytes=56 * 1024 * 1024),
        name="first_terms",
    )(inputs, gain, w_query, w_keyval)


def spread_kernel(rows_ref, weights_ref, copies_ref):
    product = jnp.dot(rows_ref[...], weights_ref[...], preferred_element_type=jnp.float32)
    product = product.astype(jnp.bfloat16)
    for at in range(copies_ref.shape[0]):
        copies_ref[at] = product


def spread_dot(rows, weights, copies):
    return pl.pallas_call(
        spread_kernel,
        out_shape=jax.ShapeDtypeStruct((copies, rows.shape[0], weights.shape[1]), jnp.bfloat16),
        compiler_params=pltpu.CompilerParams(vmem_limit_bytes=24 * 1024 * 1024),
        name="spread_dot",
    )(rows, weights)


def gateup_kernel(pair_ref, rows_ref, weights_ref, terms_ref, state_ref):
    state = (
        pair_ref[0].astype(jnp.float32) + pair_ref[1].astype(jnp.float32) + rows_ref[...].astype(jnp.float32)
    )
    state_ref[...] = state
    squares = state * state
    squares = squares[:, :128] + squares[:, 128:]
    hidden = weights_ref.shape[0]
    terms_ref[:, :, hidden:] = squares.astype(jnp.bfloat16).reshape(XS, -1, 128)
    state = state.astype(jnp.bfloat16)
    for start in range(0, hidden, 128):
        product = lax.dot_general(
            state,
            weights_ref[start : start + 128],
            (((1,), (1,)), ((), ())),
            preferred_element_type=jnp.float32,
        )
        terms_ref[:, :, start : start + 128] = product.astype(jnp.bfloat16).reshape(XS, -1, 128)


def gateup_terms(pair, rows, weights):
    count, width = rows.shape
    return pl.pallas_call(
        gateup_kernel,
        out_shape=(
            jax.ShapeDtypeStruct((XS, count // XS, weights.shape[0] + 128), jnp.bfloat16),
            jax.ShapeDtypeStruct((count, width), jnp.float32),
        ),
        compiler_params=pltpu.CompilerParams(vmem_limit_bytes=24 * 1024 * 1024),
        name="gateup_terms",
    )(pair, rows, weights)


def attend(queries, kv_cache, lengths, fresh_keys, fresh_values, score_scale):
    rows, steps, heads, head_dim = queries.shape
    merged = queries.reshape(rows, steps * heads, head_dim)
    scores = (
        jnp.einsum("rgd,rld->rgl", merged, kv_cache[..., :head_dim], preferred_element_type=jnp.float32)
        * score_scale
    )
    live = jnp.arange(kv_cache.shape[1])[None, None, :] < lengths[:, None, None]
    scores = jnp.where(live, scores, masked_score)
    fresh_scores = (
        jnp.einsum("rgd,rtd->rgt", merged, fresh_keys, preferred_element_type=jnp.float32) * score_scale
    )
    query_step = jnp.arange(steps * heads) // heads
    seen = jnp.arange(steps)[None, None, :] <= query_step[None, :, None]
    fresh_scores = jnp.where(seen, fresh_scores, masked_score)
    highest = jnp.maximum(jnp.max(scores, axis=-1), jnp.max(fresh_scores, axis=-1))[..., None]
    cache_weights = jnp.exp(scores - highest)
    fresh_weights = jnp.exp(fresh_scores - highest)
    total = jnp.sum(cache_weights, axis=-1, keepdims=True) + jnp.sum(
        fresh_weights, axis=-1, keepdims=True
    )
    cache_probs = (cache_weights / total).astype(jnp.bfloat16)
    fresh_probs = (fresh_weights / total).astype(jnp.bfloat16)
    mixed = jnp.einsum(
        "rgl,rld->rgd", cache_probs, kv_cache[..., head_dim:], preferred_element_type=jnp.float32
    ) + jnp.einsum("rgt,rtd->rgd", fresh_probs, fresh_values, preferred_element_type=jnp.float32)
    return mixed.reshape(rows, steps, heads, head_dim)


def body(
    inputs,
    attn_gain,
    w_query,
    w_keyval,
    w_out,
    ffn_gain,
    w_gateup,
    w_down,
    kv_cache,
    lengths,
    positions,
):
    steps, all_rows, local_width = inputs.shape
    local_rows = kv_cache.shape[0]
    head_dim = kv_cache.shape[3] // 2
    local_queries = w_query.shape[1] // head_dim
    local_hidden = w_down.shape[0]
    score_scale = head_dim ** (-0.5)
    keyval_weight = w_keyval.reshape(local_width, 2 * head_dim)
    keyvals_at = local_queries * head_dim
    squares_at = keyvals_at + 2 * head_dim
    rows = steps * all_rows
    x_rows = rows // XS
    terms, input_rows = first_terms(inputs, attn_gain, w_query, keyval_weight)
    sums = jnp.sum(exchange(terms, "x").astype(jnp.float32), axis=0).astype(jnp.bfloat16)
    sums, w_gateup = lax.optimization_barrier((sums, w_gateup))
    gateup = w_gateup.transpose(1, 2, 0).astype(jnp.float32) * ffn_gain.astype(jnp.float32)
    gateup = gateup.astype(jnp.bfloat16).reshape(2 * local_hidden, local_width)
    sums = exchange(sums.reshape(ZS, -1, sums.shape[1]), "z")
    sums, gateup = lax.optimization_barrier((sums, gateup))
    sums = jnp.sum(sums.astype(jnp.float32), axis=0)
    mean = jnp.sum(sums[:, squares_at:], axis=-1, keepdims=True) / D
    sums = (sums[:, :squares_at] * lax.rsqrt(mean + epsilon)).reshape(steps, local_rows, squares_at)
    offsets = positions[None, :] + jnp.arange(steps)[:, None]
    queries = rotate(
        sums[..., :keyvals_at].reshape(steps, local_rows, local_queries, head_dim), offsets[..., None]
    ).astype(jnp.bfloat16)
    keys_new = rotate(sums[..., keyvals_at : keyvals_at + head_dim], offsets).astype(jnp.bfloat16)
    values_new = sums[..., keyvals_at + head_dim :].astype(jnp.bfloat16)
    new_entries = jnp.concatenate([keys_new, values_new], axis=-1)[:, :, None, :]
    mixed = attend(
        queries.transpose(1, 0, 2, 3),
        kv_cache.reshape(local_rows, -1, 2 * head_dim),
        lengths,
        keys_new.transpose(1, 0, 2),
        values_new.transpose(1, 0, 2),
        score_scale,
    )
    heads = mixed.astype(jnp.bfloat16).transpose(1, 0, 2, 3).reshape(steps * local_rows, keyvals_at)

    all_heads = collect(collect(heads, "z", ZS).reshape(x_rows, keyvals_at), "x", XS)
    pair = group_terms(spread_dot(all_heads.reshape(rows, keyvals_at), w_out, YS))
    terms, state = gateup_terms(pair, input_rows, gateup)
    sums = jnp.sum(exchange(terms, "x").astype(jnp.float32), axis=0)
    sums = sum_over(sums, "z", ZS)
    mean = jnp.sum(sums[:, 2 * local_hidden :], axis=-1, keepdims=True) / D
    sums = sums[:, : 2 * local_hidden] * lax.rsqrt(mean + epsilon)
    activated = jax.nn.silu(sums[:, :local_hidden]) * sums[:, local_hidden:]
    hidden = collect(activated.astype(jnp.bfloat16), "z", ZS).reshape(x_rows, local_hidden)
    hidden = collect(hidden, "x", XS).reshape(rows, local_hidden)
    pair = group_terms(spread_dot(hidden, w_down, YS)).astype(jnp.float32)
    result = (pair[0] + pair[1] + state).astype(jnp.bfloat16)
    outputs = (
        result.reshape(XS * ZS, steps, local_rows, local_width)
        .transpose(1, 0, 2, 3)
        .reshape(steps, all_rows, local_width)
    )
    return (outputs, new_entries)


def solution(mesh):
    fine = Mesh(mesh.devices.reshape(XS, ZS, YS, CORES), ("x", "z", "y", "core"))
    in_specs = (
        P(None, None, WIDE),
        P(WIDE),
        P(WIDE, MP),
        P(WIDE, MP, None),
        P(MP, WIDE),
        P(WIDE),
        P(WIDE, None, MP),
        P(MP, WIDE),
        P(WIDE, None, MP, None),
        P(WIDE),
        P(WIDE),
    )
    out_specs = (P(None, None, WIDE), P(None, WIDE, MP, None))
    return jax.shard_map(body, mesh=fine, in_specs=in_specs, out_specs=out_specs, check_vma=False)
```

```python
import jax
import jax.numpy as jnp
from jax import lax
from jax.experimental import pallas as pl
from jax.experimental.pallas import tpu as pltpu
from jax.sharding import Mesh, PartitionSpec as P

D = 16384
STEPS = 2

epsilon = 1e-05
rope_base = 500000.0
masked_score = -1e30

WIDE = ("x", "z")
MP = ("y", "core")
XS, ZS, YS, CORES = 4, 16, 4, 2
QUERY_CHUNKS = 4


def angles_of(offsets, head_dim):
    half_size = head_dim // 2
    freqs = rope_base ** (-(jnp.arange(half_size, dtype=jnp.float32) * 2.0 / head_dim))
    angles = offsets.astype(jnp.float32)[..., None] * freqs
    return jnp.cos(angles), jnp.sin(angles)


def rotate(vectors, cosine, sine):
    half_size = vectors.shape[-1] // 2
    first_half = vectors[..., :half_size]
    second_half = vectors[..., half_size:]
    return jnp.concatenate(
        [first_half * cosine - second_half * sine, second_half * cosine + first_half * sine],
        axis=-1,
    )


def exchange(blocks, axis):
    return lax.all_to_all(blocks, axis, 0, 0, tiled=True)


def sum_over(terms, axis, size):
    rows, columns = terms.shape
    received = exchange(terms.astype(jnp.bfloat16).reshape(size, rows // size, columns), axis)
    return jnp.sum(received.astype(jnp.float32), axis=0)


def collect(block, axis, size):
    return exchange(jnp.broadcast_to(block[None], (size,) + block.shape), axis)


def group_terms(copies):
    total = jnp.sum(exchange(copies, "y").astype(jnp.float32), axis=0)
    return lax.all_gather(total.astype(jnp.bfloat16), "core", axis=0, tiled=False)


def to_row_order(count):
    dims = (count, count)
    mixed = lax.broadcasted_iota(jnp.int32, dims, 0)
    plain = lax.broadcasted_iota(jnp.int32, dims, 1)
    source = (mixed >> 2) * 2 + (mixed & 1) + ((mixed >> 1) & 1) * (count // 2)
    return jnp.where(source == plain, 1.0, 0.0).astype(jnp.bfloat16)


def first_kernel(
    inputs_hbm, gain_hbm, query_hbm, keyval_hbm, terms_hbm, rows_hbm,
    inputs_ref, gain_ref, query_ref, keyval_ref, terms_ref, rows_ref, sems, out_sems,
):
    group = inputs_ref.shape[1] // XS
    queries = query_ref.shape[1]
    keyvals = keyval_ref.shape[1]
    chunk = queries // QUERY_CHUNKS
    parts = [slice(chunk * at, chunk * (at + 1)) for at in range(QUERY_CHUNKS)]
    copies = [
        pltpu.make_async_copy(inputs_hbm, inputs_ref, sems.at[0]),
        pltpu.make_async_copy(gain_hbm, gain_ref, sems.at[1]),
        pltpu.make_async_copy(keyval_hbm, keyval_ref, sems.at[2]),
    ]
    for at, here in enumerate(parts):
        copies.append(pltpu.make_async_copy(query_hbm.at[:, here], query_ref.at[:, here], sems.at[3 + at]))
    for copy in copies:
        copy.start()
    order = to_row_order(2 * group)
    copies[0].wait()
    copies[1].wait()
    gain = gain_ref[...].astype(jnp.float32)[None]
    scaled = []
    for at in range(XS):
        block = jnp.concatenate([inputs_ref[step, group * at : group * (at + 1)] for step in range(2)], axis=0)
        values = jnp.dot(order, block, preferred_element_type=jnp.float32)
        rows_ref[2 * group * at : 2 * group * (at + 1)] = values.astype(jnp.bfloat16)
        squares = values * values
        terms_ref[at, :, queries + keyvals :] = (squares[:, :128] + squares[:, 128:]).astype(jnp.bfloat16)
        scaled.append((values * gain).astype(jnp.bfloat16))
    scaled = jnp.concatenate(scaled, axis=0)
    results = [pltpu.make_async_copy(rows_ref, rows_hbm, out_sems.at[0])]
    results[0].start()
    copies[2].wait()
    product = jnp.dot(scaled, keyval_ref[...], preferred_element_type=jnp.float32)
    terms_ref[:, :, queries : queries + keyvals] = product.astype(jnp.bfloat16).reshape(XS, 2 * group, keyvals)
    for at, here in enumerate([slice(queries, terms_ref.shape[2])] + parts):
        if at > 0:
            copies[2 + at].wait()
            for start in range(here.start, here.stop, 256):
                product = jnp.dot(scaled, query_ref[:, start : start + 256], preferred_element_type=jnp.float32)
                product = product.astype(jnp.bfloat16).reshape(XS, 2 * group, 256)
                terms_ref[:, :, start : start + 256] = product
        results.append(
            pltpu.make_async_copy(terms_ref.at[:, :, here], terms_hbm.at[:, :, here], out_sems.at[1 + at])
        )
        results[-1].start()
    for result in results:
        result.wait()


def first_terms(inputs, gain, w_query, w_keyval):
    steps, all_rows, width = inputs.shape
    columns = w_query.shape[1] + w_keyval.shape[1] + 128
    anywhere = pl.BlockSpec(memory_space=pl.ANY)
    terms = (XS, steps * all_rows // XS, columns)
    rows = (steps * all_rows, width)
    return pl.pallas_call(
        first_kernel,
        out_shape=(jax.ShapeDtypeStruct(terms, jnp.bfloat16), jax.ShapeDtypeStruct(rows, jnp.bfloat16)),
        in_specs=[anywhere] * 4,
        out_specs=(anywhere, anywhere),
        scratch_shapes=[
            pltpu.VMEM(inputs.shape, jnp.bfloat16),
            pltpu.VMEM(gain.shape, jnp.bfloat16),
            pltpu.VMEM(w_query.shape, jnp.bfloat16),
            pltpu.VMEM(w_keyval.shape, jnp.bfloat16),
            pltpu.VMEM(terms, jnp.bfloat16),
            pltpu.VMEM(rows, jnp.bfloat16),
            pltpu.SemaphoreType.DMA((QUERY_CHUNKS + 3,)),
            pltpu.SemaphoreType.DMA((QUERY_CHUNKS + 2,)),
        ],
        compiler_params=pltpu.CompilerParams(vmem_limit_bytes=56 * 1024 * 1024),
        name="first_terms",
    )(inputs, gain, w_query, w_keyval)


def spread_kernel(rows_ref, weights_ref, copies_ref):
    product = jnp.dot(rows_ref[...], weights_ref[...], preferred_element_type=jnp.float32)
    product = product.astype(jnp.bfloat16)
    for at in range(copies_ref.shape[0]):
        copies_ref[at] = product


def spread_dot(rows, weights, copies):
    return pl.pallas_call(
        spread_kernel,
        out_shape=jax.ShapeDtypeStruct((copies, rows.shape[0], weights.shape[1]), jnp.bfloat16),
        compiler_params=pltpu.CompilerParams(vmem_limit_bytes=24 * 1024 * 1024),
        name="spread_dot",
    )(rows, weights)


def gateup_kernel(pair_ref, rows_ref, weights_ref, terms_ref, state_ref):
    state = (
        pair_ref[0].astype(jnp.float32) + pair_ref[1].astype(jnp.float32) + rows_ref[...].astype(jnp.float32)
    )
    state_ref[...] = state
    squares = state * state
    squares = squares[:, :128] + squares[:, 128:]
    hidden = weights_ref.shape[0]
    terms_ref[:, :, hidden:] = squares.astype(jnp.bfloat16).reshape(XS, -1, 128)
    state = state.astype(jnp.bfloat16)
    for start in range(0, hidden, 128):
        product = lax.dot_general(
            state,
            weights_ref[start : start + 128],
            (((1,), (1,)), ((), ())),
            preferred_element_type=jnp.float32,
        )
        terms_ref[:, :, start : start + 128] = product.astype(jnp.bfloat16).reshape(XS, -1, 128)


def gateup_terms(pair, rows, weights):
    count, width = rows.shape
    return pl.pallas_call(
        gateup_kernel,
        out_shape=(
            jax.ShapeDtypeStruct((XS, count // XS, weights.shape[0] + 128), jnp.bfloat16),
            jax.ShapeDtypeStruct((count, width), jnp.float32),
        ),
        compiler_params=pltpu.CompilerParams(vmem_limit_bytes=24 * 1024 * 1024),
        name="gateup_terms",
    )(pair, rows, weights)


def attend(queries, kv_cache, live, fresh_keys, fresh_values, score_scale):
    rows, steps, heads, head_dim = queries.shape
    merged = queries.reshape(rows, steps * heads, head_dim)
    scores = (
        jnp.einsum("rgd,rld->rgl", merged, kv_cache[..., :head_dim], preferred_element_type=jnp.float32)
        * score_scale
    )
    scores = jnp.where(live[:, None, :] > 0.0, scores, masked_score)
    fresh_scores = (
        jnp.einsum("rgd,rtd->rgt", merged, fresh_keys, preferred_element_type=jnp.float32) * score_scale
    )
    query_step = jnp.arange(steps * heads) // heads
    seen = jnp.arange(steps)[None, None, :] <= query_step[None, :, None]
    fresh_scores = jnp.where(seen, fresh_scores, masked_score)
    highest = jnp.maximum(jnp.max(scores, axis=-1), jnp.max(fresh_scores, axis=-1))[..., None]
    cache_weights = jnp.exp(scores - highest)
    fresh_weights = jnp.exp(fresh_scores - highest)
    total = jnp.sum(cache_weights, axis=-1, keepdims=True) + jnp.sum(
        fresh_weights, axis=-1, keepdims=True
    )
    cache_probs = (cache_weights / total).astype(jnp.bfloat16)
    fresh_probs = (fresh_weights / total).astype(jnp.bfloat16)
    mixed = jnp.einsum(
        "rgl,rld->rgd", cache_probs, kv_cache[..., head_dim:], preferred_element_type=jnp.float32
    ) + jnp.einsum("rgt,rtd->rgd", fresh_probs, fresh_values, preferred_element_type=jnp.float32)
    return mixed.reshape(rows, steps, heads, head_dim)


def body(
    inputs,
    attn_gain,
    w_query,
    w_keyval,
    w_out,
    ffn_gain,
    w_gateup,
    w_down,
    kv_cache,
    lengths,
    positions,
):
    steps, all_rows, local_width = inputs.shape
    local_rows = kv_cache.shape[0]
    head_dim = kv_cache.shape[3] // 2
    local_queries = w_query.shape[1] // head_dim
    local_hidden = w_down.shape[0]
    score_scale = head_dim ** (-0.5)
    keyval_weight = w_keyval.reshape(local_width, 2 * head_dim)
    keyvals_at = local_queries * head_dim
    squares_at = keyvals_at + 2 * head_dim
    rows = steps * all_rows
    x_rows = rows // XS
    terms, input_rows = first_terms(inputs, attn_gain, w_query, keyval_weight)
    terms, w_gateup, positions, lengths = lax.optimization_barrier((terms, w_gateup, positions, lengths))
    gateup = w_gateup.transpose(1, 2, 0).astype(jnp.float32) * ffn_gain.astype(jnp.float32)
    gateup = gateup.astype(jnp.bfloat16).reshape(2 * local_hidden, local_width)
    cosine, sine = angles_of(positions[None, :] + jnp.arange(steps)[:, None], head_dim)
    live = (jnp.arange(kv_cache.shape[1])[None, :] < lengths[:, None]).astype(jnp.float32)
    sums = exchange(terms, "x")
    sums, gateup, cosine, sine, live = lax.optimization_barrier((sums, gateup, cosine, sine, live))
    sums = jnp.sum(sums.astype(jnp.float32), axis=0)
    sums = sum_over(sums, "z", ZS)
    mean = jnp.sum(sums[:, squares_at:], axis=-1, keepdims=True) / D
    sums = (sums[:, :squares_at] * lax.rsqrt(mean + epsilon)).reshape(steps, local_rows, squares_at)
    queries = rotate(
        sums[..., :keyvals_at].reshape(steps, local_rows, local_queries, head_dim),
        cosine[..., None, :],
        sine[..., None, :],
    ).astype(jnp.bfloat16)
    keys_new = rotate(sums[..., keyvals_at : keyvals_at + head_dim], cosine, sine).astype(jnp.bfloat16)
    values_new = sums[..., keyvals_at + head_dim :].astype(jnp.bfloat16)
    new_entries = jnp.concatenate([keys_new, values_new], axis=-1)[:, :, None, :]
    mixed = attend(
        queries.transpose(1, 0, 2, 3),
        kv_cache.reshape(local_rows, -1, 2 * head_dim),
        live,
        keys_new.transpose(1, 0, 2),
        values_new.transpose(1, 0, 2),
        score_scale,
    )
    heads = mixed.astype(jnp.bfloat16).transpose(1, 0, 2, 3).reshape(steps * local_rows, keyvals_at)

    all_heads = collect(collect(heads, "z", ZS).reshape(x_rows, keyvals_at), "x", XS)
    pair = group_terms(spread_dot(all_heads.reshape(rows, keyvals_at), w_out, YS))
    terms, state = gateup_terms(pair, input_rows, gateup)
    sums = jnp.sum(exchange(terms, "x").astype(jnp.float32), axis=0)
    sums = sum_over(sums, "z", ZS)
    mean = jnp.sum(sums[:, 2 * local_hidden :], axis=-1, keepdims=True) / D
    sums = sums[:, : 2 * local_hidden] * lax.rsqrt(mean + epsilon)
    activated = jax.nn.silu(sums[:, :local_hidden]) * sums[:, local_hidden:]
    hidden = collect(activated.astype(jnp.bfloat16), "z", ZS).reshape(x_rows, local_hidden)
    hidden = collect(hidden, "x", XS).reshape(rows, local_hidden)
    pair = group_terms(spread_dot(hidden, w_down, YS)).astype(jnp.float32)
    result = (pair[0] + pair[1] + state).astype(jnp.bfloat16)
    outputs = (
        result.reshape(XS * ZS, steps, local_rows, local_width)
        .transpose(1, 0, 2, 3)
        .reshape(steps, all_rows, local_width)
    )
    return (outputs, new_entries)


def solution(mesh):
    fine = Mesh(mesh.devices.reshape(XS, ZS, YS, CORES), ("x", "z", "y", "core"))
    in_specs = (
        P(None, None, WIDE),
        P(WIDE),
        P(WIDE, MP),
        P(WIDE, MP, None),
        P(MP, WIDE),
        P(WIDE),
        P(WIDE, None, MP),
        P(MP, WIDE),
        P(WIDE, None, MP, None),
        P(WIDE),
        P(WIDE),
    )
    out_specs = (P(None, None, WIDE), P(None, WIDE, MP, None))
    return jax.shard_map(body, mesh=fine, in_specs=in_specs, out_specs=out_specs, check_vma=False)
```

```python
import jax
import jax.numpy as jnp
from jax import lax
from jax.experimental import pallas as pl
from jax.experimental.pallas import tpu as pltpu
from jax.sharding import Mesh, PartitionSpec as P

D = 16384
STEPS = 2

epsilon = 1e-05
rope_base = 500000.0
masked_score = -1e30

WIDE = ("x", "z")
MP = ("y", "core")
XS, ZS, YS, CORES = 4, 16, 4, 2
QUERY_CHUNKS = 4


def rotate(vectors, offsets):
    half_size = vectors.shape[-1] // 2
    freqs = rope_base ** (-(jnp.arange(half_size, dtype=jnp.float32) * 2.0 / vectors.shape[-1]))
    angles = offsets.astype(jnp.float32)[..., None] * freqs
    cosine = jnp.cos(angles)
    sine = jnp.sin(angles)
    first_half = vectors[..., :half_size]
    second_half = vectors[..., half_size:]
    return jnp.concatenate(
        [first_half * cosine - second_half * sine, second_half * cosine + first_half * sine],
        axis=-1,
    )


def exchange(blocks, axis):
    return lax.all_to_all(blocks, axis, 0, 0, tiled=True)


def sum_over(terms, axis, size):
    rows, columns = terms.shape
    received = exchange(terms.astype(jnp.bfloat16).reshape(size, rows // size, columns), axis)
    return jnp.sum(received.astype(jnp.float32), axis=0)


def collect(block, axis, size):
    return exchange(jnp.broadcast_to(block[None], (size,) + block.shape), axis)


def group_terms(copies):
    total = jnp.sum(exchange(copies, "y").astype(jnp.float32), axis=0)
    return lax.all_gather(total.astype(jnp.bfloat16), "core", axis=0, tiled=False)


def to_row_order(count):
    dims = (count, count)
    mixed = lax.broadcasted_iota(jnp.int32, dims, 0)
    plain = lax.broadcasted_iota(jnp.int32, dims, 1)
    source = (mixed >> 2) * 2 + (mixed & 1) + ((mixed >> 1) & 1) * (count // 2)
    return jnp.where(source == plain, 1.0, 0.0).astype(jnp.bfloat16)


def first_kernel(
    inputs_hbm, gain_hbm, query_hbm, keyval_hbm, terms_hbm, rows_hbm,
    inputs_ref, gain_ref, query_ref, keyval_ref, terms_ref, rows_ref, sems, out_sems,
):
    group = inputs_ref.shape[1] // XS
    queries = query_ref.shape[1]
    keyvals = keyval_ref.shape[1]
    chunk = queries // QUERY_CHUNKS
    parts = [slice(chunk * at, chunk * (at + 1)) for at in range(QUERY_CHUNKS)]
    copies = [
        pltpu.make_async_copy(inputs_hbm, inputs_ref, sems.at[0]),
        pltpu.make_async_copy(gain_hbm, gain_ref, sems.at[1]),
        pltpu.make_async_copy(keyval_hbm, keyval_ref, sems.at[2]),
    ]
    for at, here in enumerate(parts):
        copies.append(pltpu.make_async_copy(query_hbm.at[:, here], query_ref.at[:, here], sems.at[3 + at]))
    for copy in copies:
        copy.start()
    order = to_row_order(2 * group)
    copies[0].wait()
    copies[1].wait()
    gain = gain_ref[...].astype(jnp.float32)[None]
    scaled = []
    for at in range(XS):
        block = jnp.concatenate([inputs_ref[step, group * at : group * (at + 1)] for step in range(2)], axis=0)
        values = jnp.dot(order, block, preferred_element_type=jnp.float32)
        rows_ref[2 * group * at : 2 * group * (at + 1)] = values.astype(jnp.bfloat16)
        squares = values * values
        terms_ref[at, :, queries + keyvals :] = (squares[:, :128] + squares[:, 128:]).astype(jnp.bfloat16)
        scaled.append((values * gain).astype(jnp.bfloat16))
    scaled = jnp.concatenate(scaled, axis=0)
    results = [pltpu.make_async_copy(rows_ref, rows_hbm, out_sems.at[0])]
    results[0].start()
    copies[2].wait()
    product = jnp.dot(scaled, keyval_ref[...], preferred_element_type=jnp.float32)
    terms_ref[:, :, queries : queries + keyvals] = product.astype(jnp.bfloat16).reshape(XS, 2 * group, keyvals)
    for at, here in enumerate([slice(queries, terms_ref.shape[2])] + parts):
        if at > 0:
            copies[2 + at].wait()
            for start in range(here.start, here.stop, 256):
                product = jnp.dot(scaled, query_ref[:, start : start + 256], preferred_element_type=jnp.float32)
                product = product.astype(jnp.bfloat16).reshape(XS, 2 * group, 256)
                terms_ref[:, :, start : start + 256] = product
        results.append(
            pltpu.make_async_copy(terms_ref.at[:, :, here], terms_hbm.at[:, :, here], out_sems.at[1 + at])
        )
        results[-1].start()
    for result in results:
        result.wait()


def first_terms(inputs, gain, w_query, w_keyval):
    steps, all_rows, width = inputs.shape
    columns = w_query.shape[1] + w_keyval.shape[1] + 128
    anywhere = pl.BlockSpec(memory_space=pl.ANY)
    terms = (XS, steps * all_rows // XS, columns)
    rows = (steps * all_rows, width)
    return pl.pallas_call(
        first_kernel,
        out_shape=(jax.ShapeDtypeStruct(terms, jnp.bfloat16), jax.ShapeDtypeStruct(rows, jnp.bfloat16)),
        in_specs=[anywhere] * 4,
        out_specs=(anywhere, anywhere),
        scratch_shapes=[
            pltpu.VMEM(inputs.shape, jnp.bfloat16),
            pltpu.VMEM(gain.shape, jnp.bfloat16),
            pltpu.VMEM(w_query.shape, jnp.bfloat16),
            pltpu.VMEM(w_keyval.shape, jnp.bfloat16),
            pltpu.VMEM(terms, jnp.bfloat16),
            pltpu.VMEM(rows, jnp.bfloat16),
            pltpu.SemaphoreType.DMA((QUERY_CHUNKS + 3,)),
            pltpu.SemaphoreType.DMA((QUERY_CHUNKS + 2,)),
        ],
        compiler_params=pltpu.CompilerParams(vmem_limit_bytes=56 * 1024 * 1024),
        name="first_terms",
    )(inputs, gain, w_query, w_keyval)


def parts_kernel(received_ref, blocks_ref):
    count = blocks_ref.shape[1]
    total = received_ref[0].astype(jnp.float32)
    for at in range(1, received_ref.shape[0]):
        total += received_ref[at].astype(jnp.float32)
    for at in range(blocks_ref.shape[0]):
        blocks_ref[at] = total[count * at : count * (at + 1)].astype(jnp.bfloat16)


def sum_parts(received, blocks):
    _, rows, columns = received.shape
    return pl.pallas_call(
        parts_kernel,
        out_shape=jax.ShapeDtypeStruct((blocks, rows // blocks, columns), jnp.bfloat16),
        compiler_params=pltpu.CompilerParams(vmem_limit_bytes=24 * 1024 * 1024),
        name="sum_parts",
    )(received)


def spread_kernel(rows_ref, weights_ref, copies_ref):
    product = jnp.dot(rows_ref[...], weights_ref[...], preferred_element_type=jnp.float32)
    product = product.astype(jnp.bfloat16)
    for at in range(copies_ref.shape[0]):
        copies_ref[at] = product


def spread_dot(rows, weights, copies):
    return pl.pallas_call(
        spread_kernel,
        out_shape=jax.ShapeDtypeStruct((copies, rows.shape[0], weights.shape[1]), jnp.bfloat16),
        compiler_params=pltpu.CompilerParams(vmem_limit_bytes=24 * 1024 * 1024),
        name="spread_dot",
    )(rows, weights)


def gateup_kernel(pair_ref, rows_ref, weights_ref, terms_ref, state_ref):
    state = (
        pair_ref[0].astype(jnp.float32) + pair_ref[1].astype(jnp.float32) + rows_ref[...].astype(jnp.float32)
    )
    state_ref[...] = state
    squares = state * state
    squares = squares[:, :128] + squares[:, 128:]
    hidden = weights_ref.shape[0]
    terms_ref[:, :, hidden:] = squares.astype(jnp.bfloat16).reshape(XS, -1, 128)
    state = state.astype(jnp.bfloat16)
    for start in range(0, hidden, 128):
        product = lax.dot_general(
            state,
            weights_ref[start : start + 128],
            (((1,), (1,)), ((), ())),
            preferred_element_type=jnp.float32,
        )
        terms_ref[:, :, start : start + 128] = product.astype(jnp.bfloat16).reshape(XS, -1, 128)


def gateup_terms(pair, rows, weights):
    count, width = rows.shape
    return pl.pallas_call(
        gateup_kernel,
        out_shape=(
            jax.ShapeDtypeStruct((XS, count // XS, weights.shape[0] + 128), jnp.bfloat16),
            jax.ShapeDtypeStruct((count, width), jnp.float32),
        ),
        compiler_params=pltpu.CompilerParams(vmem_limit_bytes=24 * 1024 * 1024),
        name="gateup_terms",
    )(pair, rows, weights)


def attend(queries, kv_cache, lengths, fresh_keys, fresh_values, score_scale):
    rows, steps, heads, head_dim = queries.shape
    merged = queries.reshape(rows, steps * heads, head_dim)
    scores = (
        jnp.einsum("rgd,rld->rgl", merged, kv_cache[..., :head_dim], preferred_element_type=jnp.float32)
        * score_scale
    )
    live = jnp.arange(kv_cache.shape[1])[None, None, :] < lengths[:, None, None]
    scores = jnp.where(live, scores, masked_score)
    fresh_scores = (
        jnp.einsum("rgd,rtd->rgt", merged, fresh_keys, preferred_element_type=jnp.float32) * score_scale
    )
    query_step = jnp.arange(steps * heads) // heads
    seen = jnp.arange(steps)[None, None, :] <= query_step[None, :, None]
    fresh_scores = jnp.where(seen, fresh_scores, masked_score)
    highest = jnp.maximum(jnp.max(scores, axis=-1), jnp.max(fresh_scores, axis=-1))[..., None]
    cache_weights = jnp.exp(scores - highest)
    fresh_weights = jnp.exp(fresh_scores - highest)
    total = jnp.sum(cache_weights, axis=-1, keepdims=True) + jnp.sum(
        fresh_weights, axis=-1, keepdims=True
    )
    cache_probs = (cache_weights / total).astype(jnp.bfloat16)
    fresh_probs = (fresh_weights / total).astype(jnp.bfloat16)
    mixed = jnp.einsum(
        "rgl,rld->rgd", cache_probs, kv_cache[..., head_dim:], preferred_element_type=jnp.float32
    ) + jnp.einsum("rgt,rtd->rgd", fresh_probs, fresh_values, preferred_element_type=jnp.float32)
    return mixed.reshape(rows, steps, heads, head_dim)


def body(
    inputs,
    attn_gain,
    w_query,
    w_keyval,
    w_out,
    ffn_gain,
    w_gateup,
    w_down,
    kv_cache,
    lengths,
    positions,
):
    steps, all_rows, local_width = inputs.shape
    local_rows = kv_cache.shape[0]
    head_dim = kv_cache.shape[3] // 2
    local_queries = w_query.shape[1] // head_dim
    local_hidden = w_down.shape[0]
    score_scale = head_dim ** (-0.5)
    keyval_weight = w_keyval.reshape(local_width, 2 * head_dim)
    keyvals_at = local_queries * head_dim
    squares_at = keyvals_at + 2 * head_dim
    rows = steps * all_rows
    x_rows = rows // XS
    terms, input_rows = first_terms(inputs, attn_gain, w_query, keyval_weight)
    sums = sum_parts(exchange(terms, "x"), ZS)
    sums, w_gateup = lax.optimization_barrier((sums, w_gateup))
    gateup = w_gateup.transpose(1, 2, 0).astype(jnp.float32) * ffn_gain.astype(jnp.float32)
    gateup = gateup.astype(jnp.bfloat16).reshape(2 * local_hidden, local_width)
    sums = exchange(sums, "z")
    sums, gateup = lax.optimization_barrier((sums, gateup))
    sums = jnp.sum(sums.astype(jnp.float32), axis=0)
    mean = jnp.sum(sums[:, squares_at:], axis=-1, keepdims=True) / D
    sums = (sums[:, :squares_at] * lax.rsqrt(mean + epsilon)).reshape(steps, local_rows, squares_at)
    offsets = positions[None, :] + jnp.arange(steps)[:, None]
    queries = rotate(
        sums[..., :keyvals_at].reshape(steps, local_rows, local_queries, head_dim), offsets[..., None]
    ).astype(jnp.bfloat16)
    keys_new = rotate(sums[..., keyvals_at : keyvals_at + head_dim], offsets).astype(jnp.bfloat16)
    values_new = sums[..., keyvals_at + head_dim :].astype(jnp.bfloat16)
    new_entries = jnp.concatenate([keys_new, values_new], axis=-1)[:, :, None, :]
    mixed = attend(
        queries.transpose(1, 0, 2, 3),
        kv_cache.reshape(local_rows, -1, 2 * head_dim),
        lengths,
        keys_new.transpose(1, 0, 2),
        values_new.transpose(1, 0, 2),
        score_scale,
    )
    heads = mixed.astype(jnp.bfloat16).transpose(1, 0, 2, 3).reshape(steps * local_rows, keyvals_at)

    all_heads = collect(collect(heads, "z", ZS).reshape(x_rows, keyvals_at), "x", XS)
    pair = group_terms(spread_dot(all_heads.reshape(rows, keyvals_at), w_out, YS))
    terms, state = gateup_terms(pair, input_rows, gateup)
    sums = jnp.sum(exchange(terms, "x").astype(jnp.float32), axis=0)
    sums = sum_over(sums, "z", ZS)
    mean = jnp.sum(sums[:, 2 * local_hidden :], axis=-1, keepdims=True) / D
    sums = sums[:, : 2 * local_hidden] * lax.rsqrt(mean + epsilon)
    activated = jax.nn.silu(sums[:, :local_hidden]) * sums[:, local_hidden:]
    hidden = collect(activated.astype(jnp.bfloat16), "z", ZS).reshape(x_rows, local_hidden)
    hidden = collect(hidden, "x", XS).reshape(rows, local_hidden)
    pair = group_terms(spread_dot(hidden, w_down, YS)).astype(jnp.float32)
    result = (pair[0] + pair[1] + state).astype(jnp.bfloat16)
    outputs = (
        result.reshape(XS * ZS, steps, local_rows, local_width)
        .transpose(1, 0, 2, 3)
        .reshape(steps, all_rows, local_width)
    )
    return (outputs, new_entries)


def solution(mesh):
    fine = Mesh(mesh.devices.reshape(XS, ZS, YS, CORES), ("x", "z", "y", "core"))
    in_specs = (
        P(None, None, WIDE),
        P(WIDE),
        P(WIDE, MP),
        P(WIDE, MP, None),
        P(MP, WIDE),
        P(WIDE),
        P(WIDE, None, MP),
        P(MP, WIDE),
        P(WIDE, None, MP, None),
        P(WIDE),
        P(WIDE),
    )
    out_specs = (P(None, None, WIDE), P(None, WIDE, MP, None))
    return jax.shard_map(body, mesh=fine, in_specs=in_specs, out_specs=out_specs, check_vma=False)
```

```python
import jax
import jax.numpy as jnp
from jax import lax
from jax.experimental import pallas as pl
from jax.experimental.pallas import tpu as pltpu
from jax.sharding import Mesh, PartitionSpec as P

D = 16384
STEPS = 2

epsilon = 1e-05
rope_base = 500000.0
masked_score = -1e30

WIDE = ("x", "z")
MP = ("y", "core")
XS, ZS, YS, CORES = 4, 16, 4, 2
QUERY_CHUNKS = 8


def rotate(vectors, offsets):
    half_size = vectors.shape[-1] // 2
    freqs = rope_base ** (-(jnp.arange(half_size, dtype=jnp.float32) * 2.0 / vectors.shape[-1]))
    angles = offsets.astype(jnp.float32)[..., None] * freqs
    cosine = jnp.cos(angles)
    sine = jnp.sin(angles)
    first_half = vectors[..., :half_size]
    second_half = vectors[..., half_size:]
    return jnp.concatenate(
        [first_half * cosine - second_half * sine, second_half * cosine + first_half * sine],
        axis=-1,
    )


def exchange(blocks, axis):
    return lax.all_to_all(blocks, axis, 0, 0, tiled=True)


def sum_over(terms, axis, size):
    rows, columns = terms.shape
    received = exchange(terms.astype(jnp.bfloat16).reshape(size, rows // size, columns), axis)
    return jnp.sum(received.astype(jnp.float32), axis=0)


def collect(block, axis, size):
    return exchange(jnp.broadcast_to(block[None], (size,) + block.shape), axis)


def group_terms(copies):
    total = jnp.sum(exchange(copies, "y").astype(jnp.float32), axis=0)
    return lax.all_gather(total.astype(jnp.bfloat16), "core", axis=0, tiled=False)


def to_row_order(count):
    dims = (count, count)
    mixed = lax.broadcasted_iota(jnp.int32, dims, 0)
    plain = lax.broadcasted_iota(jnp.int32, dims, 1)
    source = (mixed >> 2) * 2 + (mixed & 1) + ((mixed >> 1) & 1) * (count // 2)
    return jnp.where(source == plain, 1.0, 0.0).astype(jnp.bfloat16)


def first_kernel(
    inputs_hbm, gain_hbm, query_hbm, keyval_hbm, terms_hbm, rows_hbm,
    inputs_ref, gain_ref, query_ref, keyval_ref, terms_ref, rows_ref, sems, out_sems,
):
    group = inputs_ref.shape[1] // XS
    queries = query_ref.shape[1]
    keyvals = keyval_ref.shape[1]
    chunk = queries // QUERY_CHUNKS
    parts = [slice(chunk * at, chunk * (at + 1)) for at in range(QUERY_CHUNKS)]
    copies = [
        pltpu.make_async_copy(inputs_hbm, inputs_ref, sems.at[0]),
        pltpu.make_async_copy(gain_hbm, gain_ref, sems.at[1]),
        pltpu.make_async_copy(keyval_hbm, keyval_ref, sems.at[2]),
    ]
    for at, here in enumerate(parts):
        copies.append(pltpu.make_async_copy(query_hbm.at[:, here], query_ref.at[:, here], sems.at[3 + at]))
    for copy in copies:
        copy.start()
    order = to_row_order(2 * group)
    copies[0].wait()
    copies[1].wait()
    gain = gain_ref[...].astype(jnp.float32)[None]
    scaled = []
    for at in range(XS):
        block = jnp.concatenate([inputs_ref[step, group * at : group * (at + 1)] for step in range(2)], axis=0)
        values = jnp.dot(order, block, preferred_element_type=jnp.float32)
        rows_ref[2 * group * at : 2 * group * (at + 1)] = values.astype(jnp.bfloat16)
        squares = values * values
        terms_ref[at, :, queries + keyvals :] = (squares[:, :128] + squares[:, 128:]).astype(jnp.bfloat16)
        scaled.append((values * gain).astype(jnp.bfloat16))
    scaled = jnp.concatenate(scaled, axis=0)
    results = [pltpu.make_async_copy(rows_ref, rows_hbm, out_sems.at[0])]
    results[0].start()
    copies[2].wait()
    product = jnp.dot(scaled, keyval_ref[...], preferred_element_type=jnp.float32)
    terms_ref[:, :, queries : queries + keyvals] = product.astype(jnp.bfloat16).reshape(XS, 2 * group, keyvals)
    for at, here in enumerate([slice(queries, terms_ref.shape[2])] + parts):
        if at > 0:
            copies[2 + at].wait()
            for start in range(here.start, here.stop, 256):
                product = jnp.dot(scaled, query_ref[:, start : start + 256], preferred_element_type=jnp.float32)
                product = product.astype(jnp.bfloat16).reshape(XS, 2 * group, 256)
                terms_ref[:, :, start : start + 256] = product
        results.append(
            pltpu.make_async_copy(terms_ref.at[:, :, here], terms_hbm.at[:, :, here], out_sems.at[1 + at])
        )
        results[-1].start()
    for result in results:
        result.wait()


def first_terms(inputs, gain, w_query, w_keyval):
    steps, all_rows, width = inputs.shape
    columns = w_query.shape[1] + w_keyval.shape[1] + 128
    anywhere = pl.BlockSpec(memory_space=pl.ANY)
    terms = (XS, steps * all_rows // XS, columns)
    rows = (steps * all_rows, width)
    return pl.pallas_call(
        first_kernel,
        out_shape=(jax.ShapeDtypeStruct(terms, jnp.bfloat16), jax.ShapeDtypeStruct(rows, jnp.bfloat16)),
        in_specs=[anywhere] * 4,
        out_specs=(anywhere, anywhere),
        scratch_shapes=[
            pltpu.VMEM(inputs.shape, jnp.bfloat16),
            pltpu.VMEM(gain.shape, jnp.bfloat16),
            pltpu.VMEM(w_query.shape, jnp.bfloat16),
            pltpu.VMEM(w_keyval.shape, jnp.bfloat16),
            pltpu.VMEM(terms, jnp.bfloat16),
            pltpu.VMEM(rows, jnp.bfloat16),
            pltpu.SemaphoreType.DMA((QUERY_CHUNKS + 3,)),
            pltpu.SemaphoreType.DMA((QUERY_CHUNKS + 2,)),
        ],
        compiler_params=pltpu.CompilerParams(vmem_limit_bytes=56 * 1024 * 1024),
        name="first_terms",
    )(inputs, gain, w_query, w_keyval)


def spread_kernel(rows_ref, weights_ref, copies_ref):
    product = jnp.dot(rows_ref[...], weights_ref[...], preferred_element_type=jnp.float32)
    product = product.astype(jnp.bfloat16)
    for at in range(copies_ref.shape[0]):
        copies_ref[at] = product


def spread_dot(rows, weights, copies):
    return pl.pallas_call(
        spread_kernel,
        out_shape=jax.ShapeDtypeStruct((copies, rows.shape[0], weights.shape[1]), jnp.bfloat16),
        compiler_params=pltpu.CompilerParams(vmem_limit_bytes=24 * 1024 * 1024),
        name="spread_dot",
    )(rows, weights)


def gateup_kernel(pair_ref, rows_ref, weights_ref, terms_ref, state_ref):
    state = (
        pair_ref[0].astype(jnp.float32) + pair_ref[1].astype(jnp.float32) + rows_ref[...].astype(jnp.float32)
    )
    state_ref[...] = state
    squares = state * state
    squares = squares[:, :128] + squares[:, 128:]
    hidden = weights_ref.shape[0]
    terms_ref[:, :, hidden:] = squares.astype(jnp.bfloat16).reshape(XS, -1, 128)
    state = state.astype(jnp.bfloat16)
    for start in range(0, hidden, 128):
        product = lax.dot_general(
            state,
            weights_ref[start : start + 128],
            (((1,), (1,)), ((), ())),
            preferred_element_type=jnp.float32,
        )
        terms_ref[:, :, start : start + 128] = product.astype(jnp.bfloat16).reshape(XS, -1, 128)


def gateup_terms(pair, rows, weights):
    count, width = rows.shape
    return pl.pallas_call(
        gateup_kernel,
        out_shape=(
            jax.ShapeDtypeStruct((XS, count // XS, weights.shape[0] + 128), jnp.bfloat16),
            jax.ShapeDtypeStruct((count, width), jnp.float32),
        ),
        compiler_params=pltpu.CompilerParams(vmem_limit_bytes=24 * 1024 * 1024),
        name="gateup_terms",
    )(pair, rows, weights)


def attend(queries, kv_cache, lengths, fresh_keys, fresh_values, score_scale):
    rows, steps, heads, head_dim = queries.shape
    merged = queries.reshape(rows, steps * heads, head_dim)
    scores = (
        jnp.einsum("rgd,rld->rgl", merged, kv_cache[..., :head_dim], preferred_element_type=jnp.float32)
        * score_scale
    )
    live = jnp.arange(kv_cache.shape[1])[None, None, :] < lengths[:, None, None]
    scores = jnp.where(live, scores, masked_score)
    fresh_scores = (
        jnp.einsum("rgd,rtd->rgt", merged, fresh_keys, preferred_element_type=jnp.float32) * score_scale
    )
    query_step = jnp.arange(steps * heads) // heads
    seen = jnp.arange(steps)[None, None, :] <= query_step[None, :, None]
    fresh_scores = jnp.where(seen, fresh_scores, masked_score)
    highest = jnp.maximum(jnp.max(scores, axis=-1), jnp.max(fresh_scores, axis=-1))[..., None]
    cache_weights = jnp.exp(scores - highest)
    fresh_weights = jnp.exp(fresh_scores - highest)
    total = jnp.sum(cache_weights, axis=-1, keepdims=True) + jnp.sum(
        fresh_weights, axis=-1, keepdims=True
    )
    cache_probs = (cache_weights / total).astype(jnp.bfloat16)
    fresh_probs = (fresh_weights / total).astype(jnp.bfloat16)
    mixed = jnp.einsum(
        "rgl,rld->rgd", cache_probs, kv_cache[..., head_dim:], preferred_element_type=jnp.float32
    ) + jnp.einsum("rgt,rtd->rgd", fresh_probs, fresh_values, preferred_element_type=jnp.float32)
    return mixed.reshape(rows, steps, heads, head_dim)


def body(
    inputs,
    attn_gain,
    w_query,
    w_keyval,
    w_out,
    ffn_gain,
    w_gateup,
    w_down,
    kv_cache,
    lengths,
    positions,
):
    steps, all_rows, local_width = inputs.shape
    local_rows = kv_cache.shape[0]
    head_dim = kv_cache.shape[3] // 2
    local_queries = w_query.shape[1] // head_dim
    local_hidden = w_down.shape[0]
    score_scale = head_dim ** (-0.5)
    keyval_weight = w_keyval.reshape(local_width, 2 * head_dim)
    keyvals_at = local_queries * head_dim
    squares_at = keyvals_at + 2 * head_dim
    rows = steps * all_rows
    x_rows = rows // XS
    terms, input_rows = first_terms(inputs, attn_gain, w_query, keyval_weight)
    sums = jnp.sum(exchange(terms, "x").astype(jnp.float32), axis=0).astype(jnp.bfloat16)
    sums, w_gateup = lax.optimization_barrier((sums, w_gateup))
    gateup = w_gateup.transpose(1, 2, 0).astype(jnp.float32) * ffn_gain.astype(jnp.float32)
    gateup = gateup.astype(jnp.bfloat16).reshape(2 * local_hidden, local_width)
    sums = exchange(sums.reshape(ZS, -1, sums.shape[1]), "z")
    sums, gateup = lax.optimization_barrier((sums, gateup))
    sums = jnp.sum(sums.astype(jnp.float32), axis=0)
    mean = jnp.sum(sums[:, squares_at:], axis=-1, keepdims=True) / D
    sums = (sums[:, :squares_at] * lax.rsqrt(mean + epsilon)).reshape(steps, local_rows, squares_at)
    offsets = positions[None, :] + jnp.arange(steps)[:, None]
    queries = rotate(
        sums[..., :keyvals_at].reshape(steps, local_rows, local_queries, head_dim), offsets[..., None]
    ).astype(jnp.bfloat16)
    keys_new = rotate(sums[..., keyvals_at : keyvals_at + head_dim], offsets).astype(jnp.bfloat16)
    values_new = sums[..., keyvals_at + head_dim :].astype(jnp.bfloat16)
    new_entries = jnp.concatenate([keys_new, values_new], axis=-1)[:, :, None, :]
    mixed = attend(
        queries.transpose(1, 0, 2, 3),
        kv_cache.reshape(local_rows, -1, 2 * head_dim),
        lengths,
        keys_new.transpose(1, 0, 2),
        values_new.transpose(1, 0, 2),
        score_scale,
    )
    heads = mixed.astype(jnp.bfloat16).transpose(1, 0, 2, 3).reshape(steps * local_rows, keyvals_at)

    all_heads = collect(collect(heads, "z", ZS).reshape(x_rows, keyvals_at), "x", XS)
    pair = group_terms(spread_dot(all_heads.reshape(rows, keyvals_at), w_out, YS))
    terms, state = gateup_terms(pair, input_rows, gateup)
    sums = jnp.sum(exchange(terms, "x").astype(jnp.float32), axis=0)
    sums = sum_over(sums, "z", ZS)
    mean = jnp.sum(sums[:, 2 * local_hidden :], axis=-1, keepdims=True) / D
    sums = sums[:, : 2 * local_hidden] * lax.rsqrt(mean + epsilon)
    activated = jax.nn.silu(sums[:, :local_hidden]) * sums[:, local_hidden:]
    hidden = collect(activated.astype(jnp.bfloat16), "z", ZS).reshape(x_rows, local_hidden)
    hidden = collect(hidden, "x", XS).reshape(rows, local_hidden)
    pair = group_terms(spread_dot(hidden, w_down, YS)).astype(jnp.float32)
    result = (pair[0] + pair[1] + state).astype(jnp.bfloat16)
    outputs = (
        result.reshape(XS * ZS, steps, local_rows, local_width)
        .transpose(1, 0, 2, 3)
        .reshape(steps, all_rows, local_width)
    )
    return (outputs, new_entries)


def solution(mesh):
    fine = Mesh(mesh.devices.reshape(XS, ZS, YS, CORES), ("x", "z", "y", "core"))
    in_specs = (
        P(None, None, WIDE),
        P(WIDE),
        P(WIDE, MP),
        P(WIDE, MP, None),
        P(MP, WIDE),
        P(WIDE),
        P(WIDE, None, MP),
        P(MP, WIDE),
        P(WIDE, None, MP, None),
        P(WIDE),
        P(WIDE),
    )
    out_specs = (P(None, None, WIDE), P(None, WIDE, MP, None))
    return jax.shard_map(body, mesh=fine, in_specs=in_specs, out_specs=out_specs, check_vma=False)
```
